256 devices in a mesh: frames: 16 (over z_lo, x), verts: 16 (over y, z_hi, core).
Axes of the slice: x: 4, y: 4, z: 8 (z_hi: 2, z_lo: 4; z = z_hi * 4 + z_lo), core: 2. Of those that a mesh axis runs over, the one named last changes fastest.
Arguments:
- observed: bfloat16 [16384, 65536], P('frames', 'verts'), may hold values from -16 to 16
- mask: int32 [16384, 512], P('frames', 'verts'), may hold values 0 or 1
- basis: bfloat16 [65536, 256], P('verts'), may hold values from -6 to 6
- coeffs: float32 [16384, 256], P(('frames', 'verts')), may hold values from -6 to 6
- lag_set: int32 [8], replicated, may hold values from 1 to 32, as said below
- ar_weight: float32 [8, 256], replicated, may hold values from -0.6 to 0.6
Outputs:
- new_coeffs: float32 [16384, 256], P(('frames', 'verts'))
- new_basis: bfloat16 [65536, 256], P('verts')
The draws below stay inside these ranges and needn't reach their ends.
Inputs may be any that keep to these rules, and one draw needn't show every extreme that they name: `lag_set`: distinct lags; both 1 and 32 are among them.
All inputs are finite; a program needn't handle non-finite values. No bound on the sum of `mask` on one device may be relied on, other than what follows from the above.
Results may differ from the reference program's by a relative error of at most 0.0038.
Values may be sent and summed in bfloat16 or wider, within the bound.
A program may use at most 128 MiB of HBM per device.

```python
import jax
import jax.numpy as jnp
from jax import lax

R = 256
NLAG = 8
LAGMAX = 32
GRP = 128
FD = 1024
NF = 16384
NV = 65536


def draw_observed(key, part):
    key = jax.random.fold_in(key, 11)
    key_base, key_rough = jax.random.split(key)
    frame = jnp.arange(NF, dtype=jnp.float32) / NF
    rise = (3.0 ** frame)[:, None]
    rough = jnp.exp(jax.random.uniform(key_rough, (1, NV), jnp.float32, 0.0, 1.0986))
    base = jax.random.normal(key_base, (NF, NV), jnp.float32)
    return jnp.clip(base * rise * rough, -16.0, 16.0).astype(jnp.bfloat16)


def draw_lag_set(key, part):
    key = jax.random.fold_in(key, 23)
    middle = jax.random.permutation(key, LAGMAX - 2)[:NLAG - 2] + 2
    ends = jnp.array([1, LAGMAX], jnp.int32)
    return jnp.concatenate([ends, middle.astype(jnp.int32)])


def set_ends(result, stream_key, smallest, largest):
    longest = result.shape.index(max(result.shape))
    spots = []
    for shift in (0, 1):
        where = [jax.random.randint(jax.random.fold_in(stream_key, axis), (), 0, length) for axis, length in enumerate(result.shape)]
        where[longest] = (where[longest] + shift) % result.shape[longest]
        spots.append(tuple(where))
    return result.at[spots[0]].set(smallest).at[spots[1]].set(largest)


def shard_levels(own_key, dims, pieces, least, top_value):
    gain, own = 1.0, jax.random.fold_in(own_key, 6)
    for axis_at, parts in pieces:
        draws = jnp.exp(jax.random.uniform(jax.random.fold_in(own, axis_at), (parts,), jnp.float32, least / len(pieces), top_value / len(pieces)))
        gain = gain * jnp.repeat(draws, dims[axis_at] // parts).reshape([-1 if axis == axis_at else 1 for axis in range(len(dims))])
    return gain


def gaussian(rng, dims, spread, bound, cuts=(), held_as=jnp.bfloat16):
    entries = jax.random.normal(rng, dims, jnp.float32) * spread
    if len(cuts) > 0:
        entries = shard_levels(rng, dims, cuts, -0.22, 0.18) * entries
    return jnp.clip(entries, min=-bound, max=bound).astype(held_as)


def setup_inputs(seed: int = 0) -> dict:
    keys = jax.random.split(jax.random.key(seed), 7)
    observed = draw_observed(jax.random.fold_in(keys[6], 71), 0)
    mask = set_ends((jax.random.randint(keys[1], (NF, NV // GRP), 0, 5) < 4).astype(jnp.int32), jax.random.fold_in(keys[1], 1), 0, 1)
    basis = gaussian(keys[2], (NV, R), 1.0, 6.0, ((0, 16),))
    coeffs = gaussian(keys[3], (NF, R), 1.0, 6.0, ((0, 256),), jnp.float32)
    lag_set = draw_lag_set(jax.random.fold_in(keys[6], 71), 0)
    ar_weight = gaussian(keys[5], (NLAG, R), 0.2, 0.6, (), jnp.float32)
    return {"observed": observed, "mask": mask, "basis": basis, "coeffs": coeffs, "lag_set": lag_set, "ar_weight": ar_weight}


def residual_block(obs_block, mask_block, coeff_low, basis):
    prod = jnp.dot(coeff_low, basis.T, preferred_element_type=jnp.float32) * R ** (-0.5)
    diff = prod - obs_block.astype(jnp.float32)
    rows = diff.shape[0]
    shaped = diff.reshape(rows, mask_block.shape[1], GRP) * mask_block.astype(jnp.float32)[:, :, None]
    return shaped.reshape(rows, -1).astype(jnp.bfloat16)

def prior_grad(coeff, lag_set, ar_weight):
    total = coeff.shape[0]
    front = jnp.concatenate([jnp.zeros((LAGMAX, R), jnp.float32), coeff], axis=0)
    resid = coeff
    for index in range(NLAG):
        start = (LAGMAX - lag_set[index]).astype(jnp.int32)
        resid = resid - ar_weight[index] * lax.dynamic_slice_in_dim(front, start, total, 0)
    frame = jnp.arange(total, dtype=jnp.int32)
    resid = jnp.where((frame >= LAGMAX)[:, None], resid, jnp.zeros_like(resid))
    back = jnp.concatenate([resid, jnp.zeros((LAGMAX, R), jnp.float32)], axis=0)
    grad = resid
    for index in range(NLAG):
        start = lag_set[index].astype(jnp.int32)
        grad = grad - ar_weight[index] * lax.dynamic_slice_in_dim(back, start, total, 0)
    return grad

def reference(observed, mask, basis, coeffs, lag_set, ar_weight):
    total = coeffs.shape[0]
    blocks = total // FD
    obs_blocks = observed.reshape(blocks, FD, -1)
    mask_blocks = mask.reshape(blocks, FD, -1)
    coeff_low = coeffs.astype(jnp.bfloat16).reshape(blocks, FD, R)

    def grad_block(items):
        err = residual_block(items[0], items[1], items[2], basis)
        return jnp.dot(err, basis, preferred_element_type=jnp.float32)
    data_grad = lax.map(grad_block, (obs_blocks, mask_blocks, coeff_low)).reshape(total, R) * R ** (-0.5)
    scale_nv = basis.shape[0] ** (-0.5)
    coeff = coeffs
    for step in range(2):
        grad = data_grad * scale_nv + prior_grad(coeff, lag_set, ar_weight)
        squares = jnp.sum(grad * grad)
        coeff = coeff - 0.3 * grad / jnp.sqrt(squares / (total * R) + 1e-06)
    coeff_next = coeff.astype(jnp.bfloat16).reshape(blocks, FD, R)

    def basis_block(carry, items):
        err = residual_block(items[0], items[1], items[2], basis)
        return (carry + jnp.dot(err.T, items[2], preferred_element_type=jnp.float32), None)
    start_carry = jnp.zeros((basis.shape[0], R), jnp.float32)
    basis_grad, unused = lax.scan(basis_block, start_carry, (obs_blocks, mask_blocks, coeff_next))
    basis_grad = basis_grad * R ** (-0.5)
    new_basis = (basis.astype(jnp.float32) - 2.0 * basis_grad / jnp.sqrt(jnp.float32(total))).astype(jnp.bfloat16)
    return (coeff, new_basis)
```

```python
import jax
import jax.numpy as jnp
from jax import lax
from jax.experimental import pallas as pl
from jax.experimental.pallas import tpu as pltpu
from jax.sharding import PartitionSpec as P

R = 256
NLAG = 8
LAGMAX = 32
GRP = 128
ROWS = 1024
COLS = 4096
OWN = 64
NF = 16384
BF = jnp.bfloat16
F32 = jnp.float32
MESH = pl.DeviceIdType.MESH
NT = (((1,), (1,)), ((), ()))
WAVES = 2
WV = 512
SUB = 128


def kernel(
    obs_hbm, maskt_hbm, basis_hbm, coeff_ref, lag_ref, arw_ref,
    newc_ref, newb_hbm,
    obs, mt, mexp, basis, ag, dacc, rs_s, rs_r, ry_s, ry_r, rz_s, rz_r, zpart,
    xe, ge, px, stat1, stat2, mine,
    ct, gbuf, gown, s_opp, r_opp, s_side, r_side, s_z, r_z, nb,
    ld_sem, ag_zs, ag_zr, ag_ys, ag_yr, ag_cs, ag_cr,
    halo_s, halo_r, rc_ss, rc_rs, ry_ss, ry_rs, rz_ss, rz_rs,
    st_s, st_r, opp_s, opp_rs, side_s, side_rs, z_s, z_rs,
    az_s, az_r, ax_s, ax_r, rel_s, rel_r, out_sem,
):
    f = lax.axis_index("frames")
    v = lax.axis_index("verts")
    y, z, c = v // 4, (v // 2) % 2, v % 2
    zl, x = f // 4, f % 4
    glob = f * 16 + v
    has_prev = glob > 0
    has_next = glob < 255
    prev_dev = ((glob + 255) % 256 // 16, (glob + 255) % 16)
    next_dev = ((glob + 1) % 256 // 16, (glob + 1) % 16)

    def vdev(yy, zz, cc):
        return (f, yy * 4 + zz * 2 + cc)

    def fdev(zz, xx):
        return (zz * 4 + xx, v)

    sib = vdev(y, z, 1 - c)
    zpeer = vdev(y, 1 - z, c)
    right = fdev(zl, (x + 1) % 4)
    left = fdev(zl, (x + 3) % 4)

    def remote(src, dst, ssem, rsem, dev):
        return pltpu.make_async_remote_copy(
            src_ref=src, dst_ref=dst, send_sem=ssem, recv_sem=rsem,
            device_id=dev, device_id_type=MESH,
        )

    def load_obs(yy, cc, zz):
        return pltpu.make_async_copy(
            obs_hbm.at[pl.ds(yy * 256 + zz * 128 + cc * 64, 64)],
            obs.at[pl.ds(yy * 256 + cc * 128 + zz * 64, 64)],
            ld_sem.at[0],
        )

    def load_basis():
        return pltpu.make_async_copy(basis_hbm, basis, ld_sem.at[1])

    def load_mask():
        return pltpu.make_async_copy(maskt_hbm, mt, ld_sem.at[2])

    load_mask().start()
    load_basis().start()
    for yy in range(4):
        for cc in range(2):
            for zz in range(2):
                load_obs(yy, cc, zz).start()

    barrier = pltpu.get_barrier_semaphore()

    @pl.loop(1, 16)
    def _(d):
        pl.semaphore_signal(barrier, inc=1, device_id=(f, (v + d) % 16), device_id_type=MESH)
        pl.semaphore_signal(barrier, inc=1, device_id=((f + d) % 16, v), device_id_type=MESH)

    @pl.when(has_prev)
    def _():
        pl.semaphore_signal(barrier, inc=1, device_id=prev_dev, device_id_type=MESH)

    @pl.when(has_next)
    def _():
        pl.semaphore_signal(barrier, inc=1, device_id=next_dev, device_id_type=MESH)

    own = coeff_ref[...]
    ag[0, y, c, z] = (own.astype(BF) * 0.0625).astype(BF)
    xe[32:96] = own

    @pl.when(glob == 0)
    def _():
        xe[0:32] = jnp.zeros((32, R), F32)
        ge[0:32] = jnp.zeros((32, R), F32)

    @pl.when(glob == 255)
    def _():
        xe[96:128] = jnp.zeros((32, R), F32)
        ge[96:128] = jnp.zeros((32, R), F32)

    pl.semaphore_wait(
        barrier, 30 + has_prev.astype(jnp.int32) + has_next.astype(jnp.int32)
    )

    def ag_z(i):
        return remote(ag.at[i, y, c, z], ag.at[i, y, c, z], ag_zs.at[i], ag_zr.at[i], zpeer)

    def ag_y(i, d):
        return remote(
            ag.at[i, y, c], ag.at[i, y, c], ag_ys.at[i, d], ag_yr.at[i, d],
            vdev((y + d) % 4, z, c),
        )

    def ag_y_got(i, d):
        s = (y + 4 - d) % 4
        return remote(ag.at[i, s, c], ag.at[i, s, c], ag_ys.at[i, d], ag_yr.at[i, d], sib)

    def ag_c(i, d):
        s = (y + 4 - d) % 4
        return remote(ag.at[i, s, c], ag.at[i, s, c], ag_cs.at[i, d], ag_cr.at[i, d], sib)

    def halo(buf, i, up):
        if up:
            return remote(
                buf.at[pl.ds(64, 32)], buf.at[pl.ds(0, 32)],
                halo_s.at[i, 0], halo_r.at[i, 0], next_dev,
            )
        return remote(
            buf.at[pl.ds(32, 32)], buf.at[pl.ds(96, 32)],
            halo_s.at[i, 1], halo_r.at[i, 1], prev_dev,
        )

    def halo_start(buf, i):
        @pl.when(has_next)
        def _():
            halo(buf, i, True).start()

        @pl.when(has_prev)
        def _():
            halo(buf, i, False).start()

    def halo_wait(buf, i):
        @pl.when(has_prev)
        def _():
            halo(buf, i, True).wait_recv()

        @pl.when(has_next)
        def _():
            halo(buf, i, False).wait_recv()

    def halo_drain(buf, i):
        @pl.when(has_next)
        def _():
            halo(buf, i, True).wait_send()

        @pl.when(has_prev)
        def _():
            halo(buf, i, False).wait_send()

    def prior(buf):
        full = buf[...]
        r = full[32:128]
        for l in range(NLAG):
            r = r - arw_ref[l : l + 1, :] * pltpu.roll(full, lag_ref[l], 0)[32:128]
        frame = glob * OWN + lax.broadcasted_iota(jnp.int32, (96, R), 0)
        r = jnp.where((frame >= LAGMAX) & (frame < NF), r, 0.0)
        grad = r[0:64]
        for l in range(NLAG):
            grad = grad - arw_ref[l : l + 1, :] * pltpu.roll(r, 96 - lag_ref[l], 0)[0:64]
        return grad

    ag_z(0).start()
    halo_start(xe, 0)

    load_mask().wait()

    def expand(yy):
        for cc in range(2):
            for zz in range(2):
                src = yy * 256 + zz * 128 + cc * 64
                dst = yy * 256 + cc * 128 + zz * 64
                half = mt[:, (src // 128) * 128 : (src // 128) * 128 + 128].astype(F32).T
                m = half[cc * 64 : cc * 64 + 64]
                for g in range(32):
                    mexp[dst : dst + 64, g * 128 : (g + 1) * 128] = jnp.broadcast_to(
                        m[:, g : g + 1], (64, 128)
                    ).astype(BF)

    expand(0)
    ag_z(0).wait_recv()
    for d in range(1, 4):
        ag_y(0, d).start()
    ag_c(0, 0).start()
    for yy in range(1, 4):
        expand(yy)
    halo_wait(xe, 0)
    px[...] = prior(xe)
    load_basis().wait()
    pltpu.make_async_copy(obs_hbm, obs, ld_sem.at[0]).wait()
    for d in range(1, 4):
        ag_y_got(0, d).wait_recv()
        ag_c(0, d).start()

    def rs_core(k):
        return remote(rs_s.at[k], rs_r.at[k], rc_ss.at[k], rc_rs.at[k], sib)

    def rs_y(k):
        return remote(
            ry_s.at[k], ry_r.at[k], ry_ss.at[k], ry_rs.at[k], vdev((y + 4 - k) % 4, z, c)
        )

    @pl.loop(0, 4)
    def _(k):
        ag_c(0, k).wait_recv()
        yy = (y + 4 - k) % 4
        base = pl.multiple_of(yy * 256, 256)
        low = ag[0, yy].reshape(256, R)
        dacc[k] = jnp.zeros((256, R), F32)

        @pl.loop(0, 2)
        def _(jj):
            for u in range(2):
                cols = pl.ds(pl.multiple_of((jj * 2 + u) * 1024, 1024), 1024)
                b = basis[cols, :]
                prod = lax.dot_general(low, b, NT, preferred_element_type=F32)
                e = (prod - obs[pl.ds(base, 256), cols].astype(F32)).astype(BF) * mexp[
                    pl.ds(base, 256), cols
                ]
                dacc[k] += jnp.dot(e, b, preferred_element_type=F32)

        rs_s[k] = dacc[k, pl.ds(pl.multiple_of((1 - c) * 128, 128), 128), :].astype(BF)
        rs_core(k).start()

        @pl.when(k >= 2)
        def _():
            rs_core(k - 1).wait_recv()
            ry_s[k - 1] = (
                dacc[k - 1, pl.ds(pl.multiple_of(c * 128, 128), 128), :]
                + rs_r[k - 1].astype(F32)
            ).astype(BF)
            rs_y(k - 1).start()

    rs_core(3).wait_recv()
    ry_s[3] = (
        dacc[3, pl.ds(pl.multiple_of(c * 128, 128), 128), :] + rs_r[3].astype(F32)
    ).astype(BF)
    rs_y(3).start()
    rs_core(0).wait_recv()
    part = dacc[0, pl.ds(pl.multiple_of(c * 128, 128), 128), :] + rs_r[0].astype(F32)
    for k in range(1, 4):
        rs_y(k).wait_recv()
        part = part + ry_r[k].astype(F32)
    zpart[...] = part
    rz_s[...] = zpart[pl.ds(pl.multiple_of((1 - z) * 64, 64), 64), :].astype(BF)
    rs_z = remote(rz_s, rz_r, rz_ss, rz_rs, zpeer)
    rs_z.start()
    rs_z.wait_recv()
    total = zpart[pl.ds(pl.multiple_of(z * 64, 64), 64), :] + rz_r[...].astype(F32)

    g1 = total * (2.0 ** -12) + px[...]
    ge[32:96] = g1
    halo_start(ge, 1)
    halo_wait(ge, 1)
    pg = prior(ge)
    g1 = ge[32:96]

    def all_sum(val):
        return jnp.sum(jnp.sum(val, axis=0, keepdims=True), axis=1, keepdims=True)

    lane = lax.broadcasted_iota(jnp.int32, (1, 128), 1)
    row = jnp.where(
        lane == 0, all_sum(g1 * g1),
        jnp.where(lane == 1, all_sum(g1 * pg), jnp.where(lane == 2, all_sum(pg * pg), 0.0)),
    )

    def exchange(val, slots, i, at, dev_of):
        mine[i] = val
        slots[at] = val

        @pl.loop(1, 16)
        def _(d):
            remote(mine.at[i], slots.at[at], st_s.at[i], st_r.at[i], dev_of(d)).start()

        def whole():
            return remote(slots.at[pl.ds(0, 15)], slots.at[pl.ds(0, 15)], st_s.at[i], st_r.at[i], sib)

        whole().wait_recv()
        whole().wait_send()
        return jnp.sum(slots[...], axis=0)

    row = exchange(row, stat1, 0, v, lambda d: (f, (v + d) % 16))
    row = exchange(row, stat2, 1, f, lambda d: ((f + d) % 16, v))

    def pick(i):
        return jnp.sum(jnp.where(lane == i, row, 0.0), axis=1, keepdims=True)

    inv = 1.0 / (NF * R)
    ss1, s12, s22 = pick(0), pick(1), pick(2)
    b1 = 0.3 / jnp.sqrt(ss1 * inv + 1e-6)
    ss2 = jnp.maximum(ss1 - 2.0 * b1 * s12 + b1 * b1 * s22, 0.0)
    b2 = 0.3 / jnp.sqrt(ss2 * inv + 1e-6)
    new = coeff_ref[...] - b1 * g1 - b2 * (g1 - b1 * pg)
    newc_ref[...] = new
    ag[1, y, c, z] = (new.astype(BF) * 0.0625).astype(BF)

    ag_z(1).start()
    ag_z(1).wait_recv()
    for d in range(1, 4):
        ag_y(1, d).start()
    ag_c(1, 0).start()
    for d in range(1, 4):
        ag_y_got(1, d).wait_recv()
        ag_c(1, d).start()
    for k in range(4):
        ag_c(1, k).wait_recv()
    for yy in range(4):
        ct[:, yy * 256 : (yy + 1) * 256] = ag[1, yy].reshape(256, R).T

    def opp(w, s):
        half = pl.ds(s * 128, 128)
        return remote(
            s_opp.at[w, half], r_opp.at[w, half], opp_s.at[w, s], opp_rs.at[w, s],
            right if s == 0 else left,
        )

    def side(w, d, h):
        half = pl.ds(h * 128, 128)
        return remote(
            s_side.at[w, d, half], r_side.at[w, d, half],
            side_s.at[w, d, h], side_rs.at[w, d, h], right if d == 0 else left,
        )

    @pl.loop(0, 4 * WAVES)
    def _(n):
        w, role = n // 4, n % 4
        step = jnp.where(role == 0, 2, jnp.where(role == 1, 1, jnp.where(role == 2, 3, 0)))
        xb = (x + step) % 4
        cols = pl.ds(pl.multiple_of(xb * 1024 + w * WV, WV), WV)
        b = basis[cols, :]
        prod = lax.dot_general(ag[1].reshape(ROWS, R), b, NT, preferred_element_type=F32)
        e = (prod - obs[:, cols].astype(F32)).astype(BF) * mexp[:, cols]
        gbuf[role] = jnp.dot(ct[...], e, preferred_element_type=F32)

        @pl.when(role == 0)
        def _():
            s_opp[w] = gbuf[0].astype(BF)
            opp(w, 0).start()
            opp(w, 1).start()

        @pl.when(role == 1)
        def _():
            s_side[w, 0, 128:256] = gbuf[1, 128:256].astype(BF)
            side(w, 0, 1).start()

        @pl.when(role == 2)
        def _():
            s_side[w, 1, 0:128] = gbuf[2, 0:128].astype(BF)
            side(w, 1, 0).start()

        @pl.when(role == 3)
        def _():
            gown[w] = gbuf[3]
            opp(w, 0).wait_recv()
            s_side[w, 0, 0:128] = (gbuf[1, 0:128] + r_opp[w, 0:128].astype(F32)).astype(BF)
            side(w, 0, 0).start()
            opp(w, 1).wait_recv()
            s_side[w, 1, 128:256] = (gbuf[2, 128:256] + r_opp[w, 128:256].astype(F32)).astype(BF)
            side(w, 1, 1).start()

    def zsum(w, d):
        return remote(
            s_z.at[w, d], r_z.at[w, d], z_s.at[w, d], z_rs.at[w, d], fdev((zl + d) % 4, x)
        )

    def rows_of(xx, w, s, lo=0, n=SUB):
        return pl.ds(xx * 1024 + w * WV + s * SUB + lo, n)

    def reduce_x(w):
        for d in range(2):
            for h in range(2):
                side(w, d, h).wait_recv()
        gown[w] = gown[w] + r_side[w, 0].astype(F32) + r_side[w, 1].astype(F32)
        for d in (2, 1, 3):
            s = (zl + d) % 4
            s_z[w, d] = gown[w, :, pl.ds(pl.multiple_of(s * SUB, SUB), SUB)].astype(BF)
            zsum(w, d).start()

    def gather_z(w, d):
        rows = rows_of(x, w, zl)
        return remote(nb.at[rows], nb.at[rows], az_s.at[w, d], az_r.at[w, d], fdev((zl + d) % 4, x))

    def gather_z_got(w, d):
        rows = rows_of(x, w, (zl + 4 - d) % 4)
        return remote(nb.at[rows], nb.at[rows], az_s.at[w, d], az_r.at[w, d], left)

    def gather_x(w, d, t):
        rows = rows_of(x, w, (zl + 4 - d) % 4)
        return remote(
            nb.at[rows], nb.at[rows], ax_s.at[w, d, t], ax_r.at[w, d, t],
            right if t == 0 else left,
        )

    def gather_x_got(w, d, t):
        rows = rows_of((x + (3 if t == 0 else 1)) % 4, w, (zl + 4 - d) % 4)
        return remote(nb.at[rows], nb.at[rows], ax_s.at[w, d, t], ax_r.at[w, d, t], left)

    def relay(w, d, t):
        rows = rows_of((x + (3 if t == 0 else 1)) % 4, w, (zl + 4 - d) % 4, 64 * t, 64)
        return remote(
            nb.at[rows], nb.at[rows], rel_s.at[w, d, t], rel_r.at[w, d, t],
            right if t == 0 else left,
        )

    def relay_got(w, d, t):
        rows = rows_of((x + 2) % 4, w, (zl + 4 - d) % 4, 64 * t, 64)
        return remote(nb.at[rows], nb.at[rows], rel_s.at[w, d, t], rel_r.at[w, d, t], left)

    def update(w):
        acc = gown[w, :, pl.ds(pl.multiple_of(zl * SUB, SUB), SUB)]
        for d in range(1, 4):
            zsum(w, d).wait_recv()
            acc = acc + r_z[w, d].astype(F32)
        rows = pl.ds(pl.multiple_of(x * 1024 + w * WV + zl * SUB, SUB), SUB)
        nb[rows, :] = (basis[rows, :].astype(F32) - (2.0 ** -6) * acc.T).astype(BF)
        for d in (2, 1, 3):
            gather_z(w, d).start()
        gather_x(w, 0, 0).start()
        gather_x(w, 0, 1).start()

    def spread(w):
        for d in range(1, 4):
            gather_z_got(w, d).wait_recv()
            gather_x(w, d, 0).start()
            gather_x(w, d, 1).start()

    def pass_on(w):
        for d in range(4):
            for t in range(2):
                gather_x_got(w, d, t).wait_recv()
                relay(w, d, t).start()

    reduce_x(0)
    update(0)
    spread(0)
    reduce_x(1)
    pass_on(0)
    update(1)
    spread(1)
    pass_on(1)
    for w in range(WAVES):
        for d in range(4):
            for t in range(2):
                relay_got(w, d, t).wait_recv()
    store = pltpu.make_async_copy(nb, newb_hbm, out_sem)
    store.start()

    for i in range(2):
        ag_z(i).wait_send()
        for d in range(1, 4):
            ag_y(i, d).wait_send()
        for d in range(4):
            ag_c(i, d).wait_send()
    halo_drain(xe, 0)
    halo_drain(ge, 1)
    for k in range(4):
        rs_core(k).wait_send()
        if k:
            rs_y(k).wait_send()
    rs_z.wait_send()
    for w in range(WAVES):
        for s in range(2):
            opp(w, s).wait_send()
            for h in range(2):
                side(w, s, h).wait_send()
        for d in range(4):
            if d:
                zsum(w, d).wait_send()
                gather_z(w, d).wait_send()
            for t in range(2):
                gather_x(w, d, t).wait_send()
                relay(w, d, t).wait_send()
    store.wait()


def shards(observed, mask, basis, coeffs, lag_set, ar_weight):
    vm = pltpu.VMEM
    dma = pltpu.SemaphoreType.DMA
    scratch = [
        vm((ROWS, COLS), BF),
        vm((32, ROWS), jnp.int32),
        vm((ROWS, COLS), BF),
        vm((COLS, R), BF),
        vm((2, 4, 2, 2, OWN, R), BF),
        vm((4, 256, R), F32),
        vm((4, 128, R), BF),
        vm((4, 128, R), BF),
        vm((4, 128, R), BF),
        vm((4, 128, R), BF),
        vm((OWN, R), BF),
        vm((OWN, R), BF),
        vm((128, R), F32),
        vm((128, R), F32),
        vm((128, R), F32),
        vm((OWN, R), F32),
        vm((16, 1, 128), F32),
        vm((16, 1, 128), F32),
        vm((2, 1, 128), F32),
        vm((R, ROWS), BF),
        vm((4, R, WV), F32),
        vm((WAVES, R, WV), F32),
        vm((WAVES, R, WV), BF),
        vm((WAVES, R, WV), BF),
        vm((WAVES, 2, R, WV), BF),
        vm((WAVES, 2, R, WV), BF),
        vm((WAVES, 4, R, SUB), BF),
        vm((WAVES, 4, R, SUB), BF),
        vm((COLS, R), BF),
        dma((3,)),
        dma((2,)), dma((2,)), dma((2, 4)), dma((2, 4)), dma((2, 4)), dma((2, 4)),
        dma((2, 2)), dma((2, 2)), dma((4,)), dma((4,)), dma((4,)), dma((4,)),
        dma, dma,
        dma((2,)), dma((2,)),
        dma((WAVES, 2)), dma((WAVES, 2)), dma((WAVES, 2, 2)), dma((WAVES, 2, 2)),
        dma((WAVES, 4)), dma((WAVES, 4)), dma((WAVES, 4)), dma((WAVES, 4)),
        dma((WAVES, 4, 2)), dma((WAVES, 4, 2)), dma((WAVES, 4, 2)), dma((WAVES, 4, 2)),
        dma,
    ]
    anyspace = pl.BlockSpec(memory_space=pl.ANY)
    vmem = pl.BlockSpec(memory_space=pltpu.VMEM)
    return pl.pallas_call(
        kernel,
        out_shape=(
            jax.ShapeDtypeStruct((OWN, R), F32),
            jax.ShapeDtypeStruct((COLS, R), BF),
        ),
        in_specs=[anyspace, anyspace, anyspace, vmem, pl.BlockSpec(memory_space=pltpu.SMEM), vmem],
        out_specs=(vmem, anyspace),
        scratch_shapes=scratch,
        compiler_params=pltpu.CompilerParams(
            collective_id=0, has_side_effects=True, vmem_limit_bytes=60 * 2**20
        ),
        name="alternation",
    )(observed, mask.T, basis, coeffs, lag_set, ar_weight)


def solution(mesh):
    placed = (
        P("frames", "verts"),
        P("frames", "verts"),
        P("verts", None),
        P(("frames", "verts"), None),
        P(),
        P(),
    )
    return jax.shard_map(
        shards,
        mesh=mesh,
        in_specs=placed,
        out_specs=(P(("frames", "verts"), None), P("verts", None)),
        check_vma=False,
    )
```

```python
import jax
import jax.numpy as jnp
from jax import lax
from jax.experimental import pallas as pl
from jax.experimental.pallas import tpu as pltpu
from jax.sharding import PartitionSpec as P

R = 256
NLAG = 8
LAGMAX = 32
GRP = 128
ROWS = 1024
COLS = 4096
OWN = 64
NF = 16384
BF = jnp.bfloat16
F32 = jnp.float32
MESH = pl.DeviceIdType.MESH
NT = (((1,), (1,)), ((), ()))
WAVES = 4
WV = 256
SUB = 128


def kernel(
    obs_hbm, maskt_hbm, basis_hbm, coeff_ref, lag_ref, arw_ref,
    newc_ref, newb_hbm,
    obs, mt, mexp, basis, ag, dacc, rs_s, rs_r, ry_s, ry_r, rz_s, rz_r, zpart,
    xe, px, gfull, ghalo, pgb, cn, stat1, stat2, mine,
    ct, gacc, gown, s_opp, r_opp, s_side, r_side, s_z, r_z, nb,
    ld_sem, ag_zs, ag_zr, ag_ys, ag_yr, ag_cs, ag_cr,
    halo_s, halo_r, gh_s, gh_r, rc_ss, rc_rs, ry_ss, ry_rs, rz_ss, rz_rs,
    st_s, st_r, opp_s, opp_rs, side_s, side_rs, z_s, z_rs,
    az_s, az_r, ax_s, ax_r, rel_s, rel_r, out_sem,
):
    f = lax.axis_index("frames")
    v = lax.axis_index("verts")
    y, z, c = v // 4, (v // 2) % 2, v % 2
    zl, x = f // 4, f % 4
    glob = f * 16 + v
    has_prev = glob > 0
    has_next = glob < 255
    prev_dev = ((glob + 255) % 256 // 16, (glob + 255) % 16)
    next_dev = ((glob + 1) % 256 // 16, (glob + 1) % 16)

    below = ((f + 15) % 16, v)
    above = ((f + 1) % 16, v)

    def vdev(yy, zz, cc):
        return (f, yy * 4 + zz * 2 + cc)

    def fdev(zz, xx):
        return (zz * 4 + xx, v)

    sib = vdev(y, z, 1 - c)
    zpeer = vdev(y, 1 - z, c)
    right = fdev(zl, (x + 1) % 4)
    left = fdev(zl, (x + 3) % 4)

    def remote(src, dst, ssem, rsem, dev):
        return pltpu.make_async_remote_copy(
            src_ref=src, dst_ref=dst, send_sem=ssem, recv_sem=rsem,
            device_id=dev, device_id_type=MESH,
        )

    def load_obs(yy, cc, zz):
        return pltpu.make_async_copy(
            obs_hbm.at[pl.ds(yy * 256 + zz * 128 + cc * 64, 64)],
            obs.at[pl.ds(yy * 256 + cc * 128 + zz * 64, 64)],
            ld_sem.at[0],
        )

    def load_basis():
        return pltpu.make_async_copy(basis_hbm, basis, ld_sem.at[1])

    def load_mask():
        return pltpu.make_async_copy(maskt_hbm, mt, ld_sem.at[2])

    load_mask().start()
    load_basis().start()
    for yy in range(4):
        for cc in range(2):
            for zz in range(2):
                load_obs(yy, cc, zz).start()

    barrier = pltpu.get_barrier_semaphore()

    for d in range(1, 4):
        for dev in (vdev((y + d) % 4, z, c), fdev(zl, (x + d) % 4), fdev((zl + d) % 4, x)):
            pl.semaphore_signal(barrier, inc=1, device_id=dev, device_id_type=MESH)
    for dev in (zpeer, sib):
        pl.semaphore_signal(barrier, inc=1, device_id=dev, device_id_type=MESH)
    for has, dev in (
        (has_prev, prev_dev), (has_next, next_dev), (f > 0, below), (f < 15, above)
    ):

        @pl.when(has)
        def _():
            pl.semaphore_signal(barrier, inc=1, device_id=dev, device_id_type=MESH)

    own = coeff_ref[...]
    ag[0, y, c, z] = (own.astype(BF) * 0.0625).astype(BF)
    xe[32:96] = own

    @pl.when(glob == 0)
    def _():
        xe[0:32] = jnp.zeros((32, R), F32)

    @pl.when(glob == 255)
    def _():
        xe[96:128] = jnp.zeros((32, R), F32)

    @pl.when(f == 0)
    def _():
        ghalo[0] = jnp.zeros((32, R), BF)

    @pl.when(f == 15)
    def _():
        ghalo[1] = jnp.zeros((32, R), BF)

    def expand(k):
        yy = (y + 4 - k) % 4
        for zz in range(2):
            src = pl.multiple_of(yy * 256 + zz * 128, 128)
            m = mt[:, pl.ds(src, 128)].astype(F32).T
            for cc in range(2):
                dst = pl.multiple_of(yy * 256 + cc * 128 + zz * 64, 64)
                for g in range(32):
                    mexp[pl.ds(dst, 64), g * 128 : (g + 1) * 128] = jnp.broadcast_to(
                        m[cc * 64 : cc * 64 + 64, g : g + 1], (64, 128)
                    ).astype(BF)

    load_mask().wait()
    expand(0)
    expand(1)
    pl.semaphore_wait(
        barrier,
        11 + has_prev.astype(jnp.int32) + has_next.astype(jnp.int32)
        + (f > 0).astype(jnp.int32) + (f < 15).astype(jnp.int32),
    )

    def ag_z(i):
        return remote(ag.at[i, y, c, z], ag.at[i, y, c, z], ag_zs.at[i], ag_zr.at[i], zpeer)

    def ag_y(i, d):
        return remote(
            ag.at[i, y, c], ag.at[i, y, c], ag_ys.at[i, d], ag_yr.at[i, d],
            vdev((y + d) % 4, z, c),
        )

    def ag_y_got(i, d):
        s = (y + 4 - d) % 4
        return remote(ag.at[i, s, c], ag.at[i, s, c], ag_ys.at[i, d], ag_yr.at[i, d], sib)

    def ag_c(i, d):
        s = (y + 4 - d) % 4
        return remote(ag.at[i, s, c], ag.at[i, s, c], ag_cs.at[i, d], ag_cr.at[i, d], sib)

    def halo(up):
        if up:
            return remote(
                xe.at[pl.ds(64, 32)], xe.at[pl.ds(0, 32)], halo_s.at[0], halo_r.at[0], next_dev
            )
        return remote(
            xe.at[pl.ds(32, 32)], xe.at[pl.ds(96, 32)], halo_s.at[1], halo_r.at[1], prev_dev
        )

    def ghalo_copy(up):
        if up:
            return remote(
                ag.at[1, 3, 1, 1, pl.ds(32, 32)], ghalo.at[0], gh_s.at[0], gh_r.at[0], above
            )
        return remote(ag.at[1, 0, 0, 0, pl.ds(0, 32)], ghalo.at[1], gh_s.at[1], gh_r.at[1], below)

    def ends(copy, lower, upper, act):
        @pl.when(upper)
        def _():
            d = copy(act != "recv")
            d.start() if act == "start" else d.wait_recv() if act == "recv" else d.wait_send()

        @pl.when(lower)
        def _():
            d = copy(act == "recv")
            d.start() if act == "start" else d.wait_recv() if act == "recv" else d.wait_send()

    def prior(window, n, first):
        m = n + 32
        r = window[32:]
        for l in range(NLAG):
            r = r - arw_ref[l : l + 1, :] * pltpu.roll(window, lag_ref[l], 0)[32:]
        frame = first + lax.broadcasted_iota(jnp.int32, (m, R), 0)
        r = jnp.where((frame >= LAGMAX) & (frame < NF), r, 0.0)
        grad = r[0:n]
        for l in range(NLAG):
            grad = grad - arw_ref[l : l + 1, :] * pltpu.roll(r, m - lag_ref[l], 0)[0:n]
        return grad

    ag_z(0).start()
    ends(halo, has_prev, has_next, "start")
    ag_z(0).wait_recv()
    for d in range(1, 4):
        ag_y(0, d).start()
    ag_c(0, 0).start()
    expand(2)
    expand(3)
    ends(halo, has_prev, has_next, "recv")
    px[...] = prior(xe[...], OWN, glob * OWN)
    load_basis().wait()
    pltpu.make_async_copy(obs_hbm, obs, ld_sem.at[0]).wait()

    def rs_core(k):
        return remote(rs_s.at[k], rs_r.at[k], rc_ss.at[k], rc_rs.at[k], sib)

    def rs_y(k):
        return remote(
            ry_s.at[k], ry_r.at[k], ry_ss.at[k], ry_rs.at[k], vdev((y + 4 - k) % 4, z, c)
        )

    @pl.loop(0, 4)
    def _(k):
        ag_c(0, k).wait_recv()
        yy = (y + 4 - k) % 4
        base = pl.multiple_of(yy * 256, 256)
        low = ag[0, yy].reshape(256, R)
        dacc[k] = jnp.zeros((256, R), F32)

        @pl.loop(0, 2)
        def _(jj):
            for u in range(2):
                cols = pl.ds(pl.multiple_of((jj * 2 + u) * 1024, 1024), 1024)
                b = basis[cols, :]
                prod = lax.dot_general(low, b, NT, preferred_element_type=F32)
                e = (prod - obs[pl.ds(base, 256), cols].astype(F32)).astype(BF) * mexp[
                    pl.ds(base, 256), cols
                ]
                dacc[k] += jnp.dot(e, b, preferred_element_type=F32)

        rs_s[k] = dacc[k, pl.ds(pl.multiple_of((1 - c) * 128, 128), 128), :].astype(BF)
        rs_core(k).start()

        @pl.when(k == 0)
        def _():
            for d in range(1, 4):
                ag_y_got(0, d).wait_recv()
                ag_c(0, d).start()

        @pl.when(k >= 2)
        def _():
            rs_core(k - 1).wait_recv()
            ry_s[k - 1] = (
                dacc[k - 1, pl.ds(pl.multiple_of(c * 128, 128), 128), :]
                + rs_r[k - 1].astype(F32)
            ).astype(BF)
            rs_y(k - 1).start()

    rs_core(3).wait_recv()
    ry_s[3] = (
        dacc[3, pl.ds(pl.multiple_of(c * 128, 128), 128), :] + rs_r[3].astype(F32)
    ).astype(BF)
    rs_y(3).start()
    rs_core(0).wait_recv()
    part = dacc[0, pl.ds(pl.multiple_of(c * 128, 128), 128), :] + rs_r[0].astype(F32)
    for k in range(1, 4):
        rs_y(k).wait_recv()
        part = part + ry_r[k].astype(F32)
    zpart[...] = part * (2.0 ** -12)
    mine_rows = pl.ds(pl.multiple_of(z * 64, 64), 64)
    zpart[mine_rows, :] += px[...]
    rz_s[...] = zpart[...].astype(BF)
    rs_z = remote(rz_s, rz_r, rz_ss, rz_rs, zpeer)
    rs_z.start()
    rs_z.wait_recv()

    g128 = zpart[...] + rz_r[...].astype(F32)
    zpart[...] = g128
    ag[1, y, c] = g128.astype(BF).reshape(2, OWN, R)
    for d in range(1, 4):
        ag_y(1, d).start()
    ag_c(1, 0).start()
    for d in range(1, 4):
        ag_y_got(1, d).wait_recv()
        ag_c(1, d).start()
    for k in range(4):
        ag_c(1, k).wait_recv()
    ends(ghalo_copy, f > 0, f < 15, "start")
    for yy in range(4):
        for cc in range(2):
            for zz in range(2):
                at = 32 + yy * 256 + zz * 128 + cc * 64
                gfull[at : at + 64] = ag[1, yy, cc, zz].astype(F32)

    def fold(val):
        return jnp.sum(val, axis=0, keepdims=True)

    sums = [jnp.zeros((1, R), F32)] * 3
    for k in (1, 2, 0, 3):
        if k == 0:
            ends(ghalo_copy, f > 0, f < 15, "recv")
            gfull[0:32] = ghalo[0].astype(F32)
            gfull[1056:1088] = ghalo[1].astype(F32)
        window = gfull[k * 256 : k * 256 + 320]
        p = prior(window, 256, f * ROWS + k * 256)
        pgb[k * 256 : (k + 1) * 256] = p
        g = window[32:288]
        sums = [sums[0] + fold(g * g), sums[1] + fold(g * p), sums[2] + fold(p * p)]

    lane = lax.broadcasted_iota(jnp.int32, (1, 128), 1)
    s1, s12, s2 = [jnp.sum(t, axis=1, keepdims=True) for t in sums]
    row = jnp.where(
        lane == 0, s1, jnp.where(lane == 1, s12, jnp.where(lane == 2, s2, 0.0))
    )

    def exchange(val, slots, i, at, dev_of):
        mine[i] = val
        slots[at] = val
        for d in range(1, 4):
            remote(mine.at[i], slots.at[at], st_s.at[i], st_r.at[i], dev_of(d)).start()

        def whole():
            return remote(slots.at[pl.ds(0, 3)], slots.at[pl.ds(0, 3)], st_s.at[i], st_r.at[i], sib)

        whole().wait_recv()
        whole().wait_send()
        return jnp.sum(slots[...], axis=0)

    row = exchange(row, stat1, 0, x, lambda d: fdev(zl, (x + d) % 4))
    row = exchange(row, stat2, 1, zl, lambda d: fdev((zl + d) % 4, x))

    def pick(i):
        return jnp.sum(jnp.where(lane == i, row, 0.0), axis=1, keepdims=True)

    inv = 1.0 / (NF * R)
    ss1, s12, s22 = pick(0), pick(1), pick(2)
    b1 = 0.3 / jnp.sqrt(ss1 * inv + 1e-6)
    ss2 = jnp.maximum(ss1 - 2.0 * b1 * s12 + b1 * b1 * s22, 0.0)
    b2 = 0.3 / jnp.sqrt(ss2 * inv + 1e-6)
    by_g, by_p = b1 + b2, b1 * b2
    for yy in range(4):
        for cc in range(2):
            for zz in range(2):
                at = yy * 256 + zz * 128 + cc * 64
                low = ag[0, yy, cc, zz].astype(F32) - 0.0625 * (
                    by_g * gfull[32 + at : 96 + at] - by_p * pgb[at : at + 64]
                )
                to = yy * 256 + cc * 128 + zz * 64
                cn[to : to + 64] = low.astype(BF)
        ct[:, yy * 256 : (yy + 1) * 256] = cn[yy * 256 : (yy + 1) * 256].T
    own_at = pl.multiple_of(v * OWN, OWN)
    newc_ref[...] = (
        coeff_ref[...] - by_g * zpart[mine_rows, :] + by_p * pgb[pl.ds(own_at, OWN), :]
    )

    def opp(w, s):
        half = pl.ds(s * 128, 128)
        return remote(
            s_opp.at[w, half], r_opp.at[w, half], opp_s.at[w, s], opp_rs.at[w, s],
            right if s == 0 else left,
        )

    def side(w, d, h):
        half = pl.ds(h * 128, 128)
        return remote(
            s_side.at[w, d, half], r_side.at[w, d, half],
            side_s.at[w, d, h], side_rs.at[w, d, h], right if d == 0 else left,
        )

    def two_blocks(w, xa, xb):
        def both(ref):
            return jnp.concatenate(
                [ref[:, pl.ds(pl.multiple_of(t * 1024 + w * WV, WV), WV)] for t in (xa, xb)], axis=1
            )

        b = jnp.concatenate(
            [basis[pl.ds(pl.multiple_of(t * 1024 + w * WV, WV), WV), :] for t in (xa, xb)], axis=0
        )
        prod = lax.dot_general(cn[...], b, NT, preferred_element_type=F32)
        e = (prod - both(obs).astype(F32)).astype(BF) * both(mexp)
        return jnp.dot(ct[...], e, preferred_element_type=F32)

    def compute(w):
        g = two_blocks(w, (x + 2) % 4, (x + 1) % 4)
        s_opp[w] = g[:, 0:WV].astype(BF)
        opp(w, 0).start()
        opp(w, 1).start()
        s_side[w, 0, 128:256] = g[128:256, WV:].astype(BF)
        side(w, 0, 1).start()
        gacc[w, 0] = g[0:128, WV:]
        g = two_blocks(w, (x + 3) % 4, x)
        s_side[w, 1, 0:128] = g[0:128, 0:WV].astype(BF)
        side(w, 1, 0).start()
        gacc[w, 1] = g[128:256, 0:WV]
        gown[w] = g[:, WV:]

    def join(w):
        opp(w, 0).wait_recv()
        s_side[w, 0, 0:128] = (gacc[w, 0] + r_opp[w, 0:128].astype(F32)).astype(BF)
        side(w, 0, 0).start()
        opp(w, 1).wait_recv()
        s_side[w, 1, 128:256] = (gacc[w, 1] + r_opp[w, 128:256].astype(F32)).astype(BF)
        side(w, 1, 1).start()

    def zsum(w, d):
        return remote(
            s_z.at[w, d], r_z.at[w, d], z_s.at[w, d], z_rs.at[w, d], fdev((zl + d) % 4, x)
        )

    def quarter(s):
        return (
            pl.ds(pl.multiple_of(s // 2 * SUB, SUB), SUB),
            pl.ds(pl.multiple_of(s % 2 * SUB, SUB), SUB),
        )

    def reduce_x(w):
        for d in range(2):
            for h in range(2):
                side(w, d, h).wait_recv()
        gown[w] = gown[w] + r_side[w, 0].astype(F32) + r_side[w, 1].astype(F32)
        for d in (2, 1, 3):
            ranks, verts = quarter((zl + d) % 4)
            s_z[w, d] = gown[w, ranks, verts].astype(BF)
            zsum(w, d).start()

    def quarter_of(w, s):
        return nb.at[s // 2, pl.ds(pl.multiple_of(x * 1024 + w * WV + s % 2 * SUB, SUB), SUB)]

    def block_of(w, xx):
        return nb.at[:, pl.ds(pl.multiple_of(xx * 1024 + w * WV, WV), WV)]

    def half_of(w, xx, t):
        return nb.at[t, pl.ds(pl.multiple_of(xx * 1024 + w * WV, WV), WV)]

    def gather_z(w, d):
        part = quarter_of(w, zl)
        return remote(part, part, az_s.at[w, d], az_r.at[w, d], fdev((zl + d) % 4, x))

    def gather_z_got(w, d):
        part = quarter_of(w, (zl + 4 - d) % 4)
        return remote(part, part, az_s.at[w, d], az_r.at[w, d], left)

    def gather_x(w, t):
        part = block_of(w, x)
        return remote(part, part, ax_s.at[w, t], ax_r.at[w, t], right if t == 0 else left)

    def gather_x_got(w, t):
        part = block_of(w, (x + (3 if t == 0 else 1)) % 4)
        return remote(part, part, ax_s.at[w, t], ax_r.at[w, t], left)

    def relay(w, t):
        part = half_of(w, (x + (3 if t == 0 else 1)) % 4, t)
        return remote(part, part, rel_s.at[w, t], rel_r.at[w, t], right if t == 0 else left)

    def relay_got(w, t):
        part = half_of(w, (x + 2) % 4, t)
        return remote(part, part, rel_s.at[w, t], rel_r.at[w, t], left)

    def store(w, xx, t):
        rows = pl.ds(xx * 1024 + w * WV, WV)
        return pltpu.make_async_copy(
            nb.at[t, rows], newb_hbm.at[rows, pl.ds(t * 128, 128)], out_sem.at[w, xx, t]
        )

    def update(w):
        ranks, verts = quarter(zl)
        acc = gown[w, ranks, verts]
        for d in range(1, 4):
            zsum(w, d).wait_recv()
            acc = acc + r_z[w, d].astype(F32)
        rows = pl.ds(pl.multiple_of(x * 1024 + w * WV + zl % 2 * SUB, SUB), SUB)
        nb[zl // 2, rows, :] = (
            basis[rows, ranks].astype(F32) - (2.0 ** -6) * acc.T
        ).astype(BF)
        for d in (2, 1, 3):
            gather_z(w, d).start()

    def spread(w):
        for d in range(1, 4):
            gather_z_got(w, d).wait_recv()
        gather_x(w, 0).start()
        gather_x(w, 1).start()

    def pass_on(w):
        for t in range(2):
            gather_x_got(w, t).wait_recv()
            relay(w, t).start()

    def finish(w):
        for t in range(2):
            relay_got(w, t).wait_recv()
        for xx in range(4):
            for t in range(2):
                store(w, xx, t).start()

    for act, w in (
        (compute, 0), (compute, 1), (join, 0), (compute, 2), (join, 1), (reduce_x, 0),
        (compute, 3), (join, 2), (update, 0), (reduce_x, 1), (join, 3), (spread, 0),
        (update, 1), (reduce_x, 2), (spread, 1), (reduce_x, 3), (update, 2), (pass_on, 0),
        (update, 3), (spread, 2), (pass_on, 1), (spread, 3), (finish, 0), (pass_on, 2),
        (finish, 1), (pass_on, 3), (finish, 2), (finish, 3),
    ):
        act(w)

    ag_z(0).wait_send()
    for i in range(2):
        for d in range(1, 4):
            ag_y(i, d).wait_send()
        for d in range(4):
            ag_c(i, d).wait_send()
    ends(halo, has_prev, has_next, "send")
    ends(ghalo_copy, f > 0, f < 15, "send")
    for k in range(4):
        rs_core(k).wait_send()
        if k:
            rs_y(k).wait_send()
    rs_z.wait_send()
    for w in range(WAVES):
        for t in range(2):
            opp(w, t).wait_send()
            for h in range(2):
                side(w, t, h).wait_send()
            gather_x(w, t).wait_send()
            relay(w, t).wait_send()
        for d in range(1, 4):
            zsum(w, d).wait_send()
            gather_z(w, d).wait_send()
    for w in range(WAVES):
        for xx in range(4):
            for t in range(2):
                store(w, xx, t).wait()


def shards(observed, mask, basis, coeffs, lag_set, ar_weight):
    vm = pltpu.VMEM
    dma = pltpu.SemaphoreType.DMA
    scratch = [
        vm((ROWS, COLS), BF),
        vm((32, ROWS), jnp.int32),
        vm((ROWS, COLS), BF),
        vm((COLS, R), BF),
        vm((2, 4, 2, 2, OWN, R), BF),
        vm((4, 256, R), F32),
        vm((4, 128, R), BF),
        vm((4, 128, R), BF),
        vm((4, 128, R), BF),
        vm((4, 128, R), BF),
        vm((128, R), BF),
        vm((128, R), BF),
        vm((128, R), F32),
        vm((128, R), F32),
        vm((OWN, R), F32),
        vm((ROWS + 64, R), F32),
        vm((2, 32, R), BF),
        vm((ROWS, R), F32),
        vm((ROWS, R), BF),
        vm((4, 1, 128), F32),
        vm((4, 1, 128), F32),
        vm((2, 1, 128), F32),
        vm((R, ROWS), BF),
        vm((WAVES, 2, 128, WV), F32),
        vm((WAVES, R, WV), F32),
        vm((WAVES, R, WV), BF),
        vm((WAVES, R, WV), BF),
        vm((WAVES, 2, R, WV), BF),
        vm((WAVES, 2, R, WV), BF),
        vm((WAVES, 4, SUB, SUB), BF),
        vm((WAVES, 4, SUB, SUB), BF),
        vm((2, COLS, 128), BF),
        dma((3,)),
        dma((2,)), dma((2,)), dma((2, 4)), dma((2, 4)), dma((2, 4)), dma((2, 4)),
        dma((2,)), dma((2,)), dma((2,)), dma((2,)),
        dma((4,)), dma((4,)), dma((4,)), dma((4,)), dma, dma,
        dma((2,)), dma((2,)),
        dma((WAVES, 2)), dma((WAVES, 2)), dma((WAVES, 2, 2)), dma((WAVES, 2, 2)),
        dma((WAVES, 4)), dma((WAVES, 4)), dma((WAVES, 4)), dma((WAVES, 4)),
        dma((WAVES, 2)), dma((WAVES, 2)), dma((WAVES, 2)), dma((WAVES, 2)),
        dma((WAVES, 4, 2)),
    ]
    anyspace = pl.BlockSpec(memory_space=pl.ANY)
    vmem = pl.BlockSpec(memory_space=pltpu.VMEM)
    return pl.pallas_call(
        kernel,
        out_shape=(
            jax.ShapeDtypeStruct((OWN, R), F32),
            jax.ShapeDtypeStruct((COLS, R), BF),
        ),
        in_specs=[anyspace, anyspace, anyspace, vmem, pl.BlockSpec(memory_space=pltpu.SMEM), vmem],
        out_specs=(vmem, anyspace),
        scratch_shapes=scratch,
        compiler_params=pltpu.CompilerParams(
            collective_id=0, has_side_effects=True, vmem_limit_bytes=60 * 2**20
        ),
        name="alternation",
    )(observed, mask.T, basis, coeffs, lag_set, ar_weight)


def solution(mesh):
    placed = (
        P("frames", "verts"),
        P("frames", "verts"),
        P("verts", None),
        P(("frames", "verts"), None),
        P(),
        P(),
    )
    return jax.shard_map(
        shards,
        mesh=mesh,
        in_specs=placed,
        out_specs=(P(("frames", "verts"), None), P("verts", None)),
        check_vma=False,
    )
```

```python
import jax
import jax.numpy as jnp
from jax import lax
from jax.experimental import pallas as pl
from jax.experimental.pallas import tpu as pltpu
from jax.sharding import PartitionSpec as P

R = 256
NLAG = 8
LAGMAX = 32
GRP = 128
ROWS = 1024
COLS = 4096
OWN = 64
NF = 16384
BF = jnp.bfloat16
F32 = jnp.float32
MESH = pl.DeviceIdType.MESH
NT = (((1,), (1,)), ((), ()))
WAVES = 4
WV = 256
SUB = 128


def kernel(
    obs_hbm, maskt_hbm, basis_hbm, coeff_ref, lag_ref, arw_ref,
    newc_ref, newb_hbm,
    obs, mt, mexp, basis, ag, dacc, rs_s, rs_r, ry_s, ry_r, rz_s, rz_r, zpart,
    xe, px, gfull, ghalo, rbuf, sums, pgb, cn, stat1, stat2, mine,
    ct, gacc, gown, s_opp, r_opp, s_side, r_side, s_near, r_near, s_far, r_far, nb,
    ld_sem, ag_zs, ag_zr, ag_ys, ag_yr, ag_cs, ag_cr,
    halo_s, halo_r, gh_s, gh_r, rc_ss, rc_rs, ry_ss, ry_rs, rz_ss, rz_rs,
    st_s, st_r, opp_s, opp_rs, side_s, side_rs, z_s, z_rs,
    az_s, az_r, ax_s, ax_r, rel_s, rel_r, out_sem,
):
    f = lax.axis_index("frames")
    v = lax.axis_index("verts")
    y, z, c = v // 4, (v // 2) % 2, v % 2
    zl, x = f // 4, f % 4
    glob = f * 16 + v
    has_prev = glob > 0
    has_next = glob < 255
    prev_dev = ((glob + 255) % 256 // 16, (glob + 255) % 16)
    next_dev = ((glob + 1) % 256 // 16, (glob + 1) % 16)

    below = ((f + 15) % 16, v)
    above = ((f + 1) % 16, v)

    def vdev(yy, zz, cc):
        return (f, yy * 4 + zz * 2 + cc)

    def fdev(zz, xx):
        return (zz * 4 + xx, v)

    sib = vdev(y, z, 1 - c)
    zpeer = vdev(y, 1 - z, c)
    right = fdev(zl, (x + 1) % 4)
    left = fdev(zl, (x + 3) % 4)

    def remote(src, dst, ssem, rsem, dev):
        return pltpu.make_async_remote_copy(
            src_ref=src, dst_ref=dst, send_sem=ssem, recv_sem=rsem,
            device_id=dev, device_id_type=MESH,
        )

    def load_obs(yy, cc, zz):
        return pltpu.make_async_copy(
            obs_hbm.at[pl.ds(yy * 256 + zz * 128 + cc * 64, 64)],
            obs.at[pl.ds(yy * 256 + cc * 128 + zz * 64, 64)],
            ld_sem.at[0],
        )

    def load_basis():
        return pltpu.make_async_copy(basis_hbm, basis, ld_sem.at[1])

    def load_mask():
        return pltpu.make_async_copy(maskt_hbm, mt, ld_sem.at[2])

    load_mask().start()
    load_basis().start()
    for yy in range(4):
        for cc in range(2):
            for zz in range(2):
                load_obs(yy, cc, zz).start()

    barrier = pltpu.get_barrier_semaphore()

    for d in range(1, 4):
        for dev in (vdev((y + d) % 4, z, c), fdev(zl, (x + d) % 4), fdev((zl + d) % 4, x)):
            pl.semaphore_signal(barrier, inc=1, device_id=dev, device_id_type=MESH)
    for dev in (zpeer, sib):
        pl.semaphore_signal(barrier, inc=1, device_id=dev, device_id_type=MESH)
    for has, dev in (
        (has_prev, prev_dev), (has_next, next_dev), (f > 0, below), (f < 15, above)
    ):

        @pl.when(has)
        def _():
            pl.semaphore_signal(barrier, inc=1, device_id=dev, device_id_type=MESH)

    own = coeff_ref[...]
    ag[0, y, c, z] = (own.astype(BF) * 0.0625).astype(BF)
    xe[32:96] = own

    @pl.when(glob == 0)
    def _():
        xe[0:32] = jnp.zeros((32, R), F32)

    @pl.when(glob == 255)
    def _():
        xe[96:128] = jnp.zeros((32, R), F32)

    @pl.when(f == 0)
    def _():
        ghalo[0] = jnp.zeros((32, R), BF)

    @pl.when(f == 15)
    def _():
        ghalo[1] = jnp.zeros((32, R), BF)

    def expand(k):
        yy = (y + 4 - k) % 4
        for zz in range(2):
            src = pl.multiple_of(yy * 256 + zz * 128, 128)
            m = mt[:, pl.ds(src, 128)].astype(F32).T
            for cc in range(2):
                dst = pl.multiple_of(yy * 256 + cc * 128 + zz * 64, 64)
                for g in range(32):
                    mexp[pl.ds(dst, 64), g * 128 : (g + 1) * 128] = jnp.broadcast_to(
                        m[cc * 64 : cc * 64 + 64, g : g + 1], (64, 128)
                    ).astype(BF)

    load_mask().wait()
    pl.loop(0, 2)(expand)
    pl.semaphore_wait(
        barrier,
        11 + has_prev.astype(jnp.int32) + has_next.astype(jnp.int32)
        + (f > 0).astype(jnp.int32) + (f < 15).astype(jnp.int32),
    )

    def ag_z(i):
        return remote(ag.at[i, y, c, z], ag.at[i, y, c, z], ag_zs.at[i], ag_zr.at[i], zpeer)

    def ag_y(i, d):
        return remote(
            ag.at[i, y, c], ag.at[i, y, c], ag_ys.at[i, d], ag_yr.at[i, d],
            vdev((y + d) % 4, z, c),
        )

    def ag_y_got(i, d):
        s = (y + 4 - d) % 4
        return remote(ag.at[i, s, c], ag.at[i, s, c], ag_ys.at[i, d], ag_yr.at[i, d], sib)

    def ag_c(i, d):
        s = (y + 4 - d) % 4
        return remote(ag.at[i, s, c], ag.at[i, s, c], ag_cs.at[i, d], ag_cr.at[i, d], sib)

    def halo(up):
        if up:
            return remote(
                xe.at[pl.ds(64, 32)], xe.at[pl.ds(0, 32)], halo_s.at[0], halo_r.at[0], next_dev
            )
        return remote(
            xe.at[pl.ds(32, 32)], xe.at[pl.ds(96, 32)], halo_s.at[1], halo_r.at[1], prev_dev
        )

    def ghalo_copy(up):
        if up:
            return remote(
                ag.at[1, 3, 1, 1, pl.ds(32, 32)], ghalo.at[0], gh_s.at[0], gh_r.at[0], above
            )
        return remote(ag.at[1, 0, 0, 0, pl.ds(0, 32)], ghalo.at[1], gh_s.at[1], gh_r.at[1], below)

    def ends(copy, lower, upper, act):
        @pl.when(upper)
        def _():
            d = copy(act != "recv")
            d.start() if act == "start" else d.wait_recv() if act == "recv" else d.wait_send()

        @pl.when(lower)
        def _():
            d = copy(act == "recv")
            d.start() if act == "start" else d.wait_recv() if act == "recv" else d.wait_send()

    def prior(window, n, first):
        m = n + 32
        r = window[32:]
        for l in range(NLAG):
            r = r - arw_ref[l : l + 1, :] * pltpu.roll(window, lag_ref[l], 0)[32:]
        frame = first + lax.broadcasted_iota(jnp.int32, (m, R), 0)
        r = jnp.where((frame >= LAGMAX) & (frame < NF), r, 0.0)
        grad = r[0:n]
        for l in range(NLAG):
            grad = grad - arw_ref[l : l + 1, :] * pltpu.roll(r, m - lag_ref[l], 0)[0:n]
        return grad

    ag_z(0).start()
    ends(halo, has_prev, has_next, "start")
    ag_z(0).wait_recv()
    for d in range(1, 4):
        ag_y(0, d).start()
    ag_c(0, 0).start()
    pl.loop(2, 4)(expand)
    ends(halo, has_prev, has_next, "recv")
    px[...] = prior(xe[...], OWN, glob * OWN)
    load_basis().wait()
    pltpu.make_async_copy(obs_hbm, obs, ld_sem.at[0]).wait()

    def rs_core(k):
        return remote(rs_s.at[k], rs_r.at[k], rc_ss.at[k], rc_rs.at[k], sib)

    def rs_y(k):
        return remote(
            ry_s.at[k], ry_r.at[k], ry_ss.at[k], ry_rs.at[k], vdev((y + 4 - k) % 4, z, c)
        )

    @pl.loop(0, 4)
    def _(k):
        ag_c(0, k).wait_recv()
        yy = (y + 4 - k) % 4
        base = pl.multiple_of(yy * 256, 256)
        low = ag[0, yy].reshape(256, R)
        dacc[k] = jnp.zeros((256, R), F32)

        @pl.loop(0, 2)
        def _(jj):
            for u in range(2):
                cols = pl.ds(pl.multiple_of((jj * 2 + u) * 1024, 1024), 1024)
                b = basis[cols, :]
                prod = lax.dot_general(low, b, NT, preferred_element_type=F32)
                e = (prod - obs[pl.ds(base, 256), cols].astype(F32)).astype(BF) * mexp[
                    pl.ds(base, 256), cols
                ]
                dacc[k] += jnp.dot(e, b, preferred_element_type=F32)

        rs_s[k] = dacc[k, pl.ds(pl.multiple_of((1 - c) * 128, 128), 128), :].astype(BF)
        rs_core(k).start()

        @pl.when(k == 0)
        def _():
            for d in range(1, 4):
                ag_y_got(0, d).wait_recv()
                ag_c(0, d).start()

        @pl.when(k >= 2)
        def _():
            rs_core(k - 1).wait_recv()
            ry_s[k - 1] = (
                dacc[k - 1, pl.ds(pl.multiple_of(c * 128, 128), 128), :]
                + rs_r[k - 1].astype(F32)
            ).astype(BF)
            rs_y(k - 1).start()

    rs_core(3).wait_recv()
    ry_s[3] = (
        dacc[3, pl.ds(pl.multiple_of(c * 128, 128), 128), :] + rs_r[3].astype(F32)
    ).astype(BF)
    rs_y(3).start()
    rs_core(0).wait_recv()
    part = dacc[0, pl.ds(pl.multiple_of(c * 128, 128), 128), :] + rs_r[0].astype(F32)
    for k in range(1, 4):
        rs_y(k).wait_recv()
        part = part + ry_r[k].astype(F32)
    zpart[...] = part * (2.0 ** -12)
    mine_rows = pl.ds(pl.multiple_of(z * 64, 64), 64)
    zpart[mine_rows, :] += px[...]
    rz_s[...] = zpart[...].astype(BF)
    rs_z = remote(rz_s, rz_r, rz_ss, rz_rs, zpeer)
    rs_z.start()
    rs_z.wait_recv()

    g128 = zpart[...] + rz_r[...].astype(F32)
    zpart[...] = g128
    ag[1, y, c] = g128.astype(BF).reshape(2, OWN, R)
    for d in range(1, 4):
        ag_y(1, d).start()
    ag_c(1, 0).start()
    for d in range(1, 4):
        ag_y_got(1, d).wait_recv()
        ag_c(1, d).start()
    for k in range(4):
        ag_c(1, k).wait_recv()
    ends(ghalo_copy, f > 0, f < 15, "start")
    def blocks(act):
        @pl.loop(0, 4)
        def _(yy):
            for cc in range(2):
                for zz in range(2):
                    frame = pl.multiple_of(yy * 256 + zz * 128 + cc * 64, 64)
                    place = pl.multiple_of(yy * 256 + cc * 128 + zz * 64, 64)
                    act(yy, cc, zz, frame, place)

    def widen(yy, cc, zz, frame, place):
        gfull[pl.ds(40 + frame, OWN), :] = ag[1, yy, cc, zz].astype(F32)

    blocks(widen)
    sub8 = lax.broadcasted_iota(jnp.int32, (1, 8, R), 1)

    def moved(turned, tiles):
        n = turned.shape[0] - 4
        a = jnp.where((tiles & 1) == 1, turned[1:], turned[:-1])
        a = jnp.where((tiles & 2) == 2, a[2:], a[:-2])
        return jnp.where(tiles == 4, turned[4:], a[:n]).reshape(n * 8, R)

    def earlier(window, lag):
        low = lag & 7
        turned = pltpu.roll(window, low, 1)
        near_rows = jnp.where(sub8 >= low, turned[1:], turned[:-1])
        return moved(near_rows, 4 - ((sub8 * 0 + lag) >> 3))

    def later(window, lag):
        low = lag & 7
        turned = pltpu.roll(window, (8 - low) & 7, 1)
        near_rows = jnp.where(sub8 < 8 - low, turned[:-1], turned[1:])
        return moved(near_rows, (sub8 * 0 + lag) >> 3)

    gfull[0:8] = jnp.zeros((8, R), F32)
    rbuf[1056:1064] = jnp.zeros((8, R), F32)

    @pl.loop(0, 11)
    def _(i):
        @pl.when(i == 9)
        def _():
            ends(ghalo_copy, f > 0, f < 15, "recv")
            gfull[8:40] = ghalo[0].astype(F32)
            gfull[1064:1096] = ghalo[1].astype(F32)

        at = pl.multiple_of((i + 1) % 11 * 96, 8)
        window = gfull[pl.ds(at, 136), :].reshape(17, 8, R)
        r = gfull[pl.ds(40 + at, 96), :]
        for l in range(NLAG):
            r = r - arw_ref[l : l + 1, :] * earlier(window, lag_ref[l])
        frame = f * ROWS + at + lax.broadcasted_iota(jnp.int32, (96, R), 0)
        rbuf[pl.ds(at, 96), :] = jnp.where((frame >= LAGMAX) & (frame < NF), r, 0.0)

    sums[...] = jnp.zeros_like(sums)

    @pl.loop(0, 8)
    def _(i):
        at = pl.multiple_of(i * 128, 128)
        window = rbuf[pl.ds(at, 168), :].reshape(21, 8, R)
        p = rbuf[pl.ds(at, 128), :]
        for l in range(NLAG):
            p = p - arw_ref[l : l + 1, :] * later(window, lag_ref[l])
        pgb[pl.ds(at, 128), :] = p
        g = gfull[pl.ds(40 + at, 128), :]
        for n, val in enumerate((g * g, g * p, p * p)):
            sums[n] += jnp.sum(val.reshape(16, 8, R), axis=0)

    lane = lax.broadcasted_iota(jnp.int32, (1, 128), 1)
    s1, s12, s2 = [
        jnp.sum(jnp.sum(sums[n], axis=0, keepdims=True), axis=1, keepdims=True) for n in range(3)
    ]
    row = jnp.where(
        lane == 0, s1, jnp.where(lane == 1, s12, jnp.where(lane == 2, s2, 0.0))
    )

    def exchange(val, slots, i, at, dev_of):
        mine[i] = val
        slots[at] = val
        for d in range(1, 4):
            remote(mine.at[i], slots.at[at], st_s.at[i], st_r.at[i], dev_of(d)).start()

        def whole():
            return remote(slots.at[pl.ds(0, 3)], slots.at[pl.ds(0, 3)], st_s.at[i], st_r.at[i], sib)

        whole().wait_recv()
        whole().wait_send()
        return jnp.sum(slots[...], axis=0)

    row = exchange(row, stat1, 0, x, lambda d: fdev(zl, (x + d) % 4))
    row = exchange(row, stat2, 1, zl, lambda d: fdev((zl + d) % 4, x))

    def pick(i):
        return jnp.sum(jnp.where(lane == i, row, 0.0), axis=1, keepdims=True)

    inv = 1.0 / (NF * R)
    ss1, s12, s22 = pick(0), pick(1), pick(2)
    b1 = 0.3 / jnp.sqrt(ss1 * inv + 1e-6)
    ss2 = jnp.maximum(ss1 - 2.0 * b1 * s12 + b1 * b1 * s22, 0.0)
    b2 = 0.3 / jnp.sqrt(ss2 * inv + 1e-6)
    by_g, by_p = b1 + b2, b1 * b2
    def step(yy, cc, zz, frame, place):
        low = ag[0, yy, cc, zz].astype(F32) - 0.0625 * (
            by_g * gfull[pl.ds(40 + frame, OWN), :] - by_p * pgb[pl.ds(frame, OWN), :]
        )
        cn[pl.ds(place, OWN), :] = low.astype(BF)

    blocks(step)

    @pl.loop(0, 4)
    def _(yy):
        at = pl.multiple_of(yy * 256, 256)
        ct[:, pl.ds(at, 256)] = cn[pl.ds(at, 256), :].T

    own_at = pl.multiple_of(v * OWN, OWN)
    newc_ref[...] = (
        coeff_ref[...] - by_g * zpart[mine_rows, :] + by_p * pgb[pl.ds(own_at, OWN), :]
    )

    def opp(w, s):
        half = pl.ds(s * 128, 128)
        return remote(
            s_opp.at[w, half], r_opp.at[w, half], opp_s.at[w, s], opp_rs.at[w, s],
            right if s == 0 else left,
        )

    def side(w, d, h):
        half = pl.ds(h * 128, 128)
        return remote(
            s_side.at[w, d, half], r_side.at[w, d, half],
            side_s.at[w, d, h], side_rs.at[w, d, h], right if d == 0 else left,
        )

    def two_blocks(w, xa, xb):
        def both(ref):
            return jnp.concatenate(
                [ref[:, pl.ds(pl.multiple_of(t * 1024 + w * WV, WV), WV)] for t in (xa, xb)], axis=1
            )

        b = jnp.concatenate(
            [basis[pl.ds(pl.multiple_of(t * 1024 + w * WV, WV), WV), :] for t in (xa, xb)], axis=0
        )
        prod = lax.dot_general(cn[...], b, NT, preferred_element_type=F32)
        e = (prod - both(obs).astype(F32)).astype(BF) * both(mexp)
        return jnp.dot(ct[...], e, preferred_element_type=F32)

    def compute(w):
        g = two_blocks(w, (x + 2) % 4, (x + 1) % 4)
        s_opp[w] = g[:, 0:WV].astype(BF)
        opp(w, 0).start()
        opp(w, 1).start()
        s_side[w, 0, 128:256] = g[128:256, WV:].astype(BF)
        side(w, 0, 1).start()
        gacc[w, 0] = g[0:128, WV:]
        g = two_blocks(w, (x + 3) % 4, x)
        s_side[w, 1, 0:128] = g[0:128, 0:WV].astype(BF)
        side(w, 1, 0).start()
        gacc[w, 1] = g[128:256, 0:WV]
        gown[w] = g[:, WV:]

    def join(w):
        opp(w, 0).wait_recv()
        s_side[w, 0, 0:128] = (gacc[w, 0] + r_opp[w, 0:128].astype(F32)).astype(BF)
        side(w, 0, 0).start()
        opp(w, 1).wait_recv()
        s_side[w, 1, 128:256] = (gacc[w, 1] + r_opp[w, 128:256].astype(F32)).astype(BF)
        side(w, 1, 1).start()

    near, far = fdev(zl // 2 * 2 + 1 - zl % 2, x), fdev((zl + 2) % 4, x)

    def to_near(w):
        return remote(s_near.at[w], r_near.at[w], z_s.at[w, 0], z_rs.at[w, 0], near)

    def to_far(w):
        return remote(s_far.at[w], r_far.at[w], z_s.at[w, 1], z_rs.at[w, 1], far)

    def of(i):
        return pl.ds(pl.multiple_of(i * SUB, SUB), SUB)

    def reduce_x(w):
        for d in range(2):
            for h in range(2):
                side(w, d, h).wait_recv()
        gown[w] = gown[w] + r_side[w, 0].astype(F32) + r_side[w, 1].astype(F32)
        s_near[w] = gown[w, :, of(1 - zl % 2)].astype(BF)
        to_near(w).start()

    def reduce_near(w):
        to_near(w).wait_recv()
        mine_verts = of(zl % 2)
        gown[w, :, mine_verts] = gown[w, :, mine_verts] + r_near[w].astype(F32)
        s_far[w] = gown[w, of(1 - zl // 2), mine_verts].astype(BF)
        to_far(w).start()

    def eighth_of(w, i):
        return pl.ds(pl.multiple_of(x * 1024 + w * WV + i * SUB, SUB), SUB)

    def block_of(w, xx):
        return nb.at[:, pl.ds(pl.multiple_of(xx * 1024 + w * WV, WV), WV)]

    def half_of(w, xx, t):
        return nb.at[t, pl.ds(pl.multiple_of(xx * 1024 + w * WV, WV), WV)]

    def gather_far(w, got):
        part = nb.at[1 - zl // 2 if got else zl // 2, eighth_of(w, zl % 2)]
        return remote(part, part, az_s.at[w, 0], az_r.at[w, 0], far)

    def gather_near(w, got):
        part = nb.at[:, eighth_of(w, 1 - zl % 2 if got else zl % 2)]
        return remote(part, part, az_s.at[w, 1], az_r.at[w, 1], near)

    def gather_x(w, t):
        part = block_of(w, x)
        return remote(part, part, ax_s.at[w, t], ax_r.at[w, t], right if t == 0 else left)

    def gather_x_got(w, t):
        part = block_of(w, (x + (3 if t == 0 else 1)) % 4)
        return remote(part, part, ax_s.at[w, t], ax_r.at[w, t], left)

    def relay(w, t):
        part = half_of(w, (x + (3 if t == 0 else 1)) % 4, t)
        return remote(part, part, rel_s.at[w, t], rel_r.at[w, t], right if t == 0 else left)

    def relay_got(w, t):
        part = half_of(w, (x + 2) % 4, t)
        return remote(part, part, rel_s.at[w, t], rel_r.at[w, t], left)

    def store(w, xx, t):
        rows = pl.ds(xx * 1024 + w * WV, WV)
        return pltpu.make_async_copy(
            nb.at[t, rows], newb_hbm.at[rows, pl.ds(t * 128, 128)], out_sem.at[w, xx, t]
        )

    def update(w):
        to_far(w).wait_recv()
        ranks = of(zl // 2)
        acc = gown[w, ranks, of(zl % 2)] + r_far[w].astype(F32)
        rows = eighth_of(w, zl % 2)
        nb[zl // 2, rows, :] = (
            basis[rows, ranks].astype(F32) - (2.0 ** -6) * acc.T
        ).astype(BF)
        gather_far(w, False).start()

    def spread_near(w):
        gather_far(w, True).wait_recv()
        gather_near(w, False).start()

    def spread(w):
        gather_near(w, True).wait_recv()
        gather_x(w, 0).start()
        gather_x(w, 1).start()

    def pass_on(w):
        for t in range(2):
            gather_x_got(w, t).wait_recv()
            relay(w, t).start()

    def finish(w):
        for t in range(2):
            relay_got(w, t).wait_recv()
        for xx in range(4):
            for t in range(2):
                store(w, xx, t).start()

    @pl.loop(0, WAVES + 8)
    def _(t):
        for act, behind in (
            (compute, 0), (join, 1), (spread_near, 5), (update, 4), (spread, 5),
            (reduce_near, 3), (reduce_x, 2), (pass_on, 6), (finish, 8),
        ):

            @pl.when((t >= behind) & (t < WAVES + behind))
            def _():
                act(t - behind)

    ag_z(0).wait_send()
    for i in range(2):
        for d in range(1, 4):
            ag_y(i, d).wait_send()
        for d in range(4):
            ag_c(i, d).wait_send()
    ends(halo, has_prev, has_next, "send")
    ends(ghalo_copy, f > 0, f < 15, "send")
    for k in range(4):
        rs_core(k).wait_send()
        if k:
            rs_y(k).wait_send()
    rs_z.wait_send()
    for w in range(WAVES):
        for t in range(2):
            opp(w, t).wait_send()
            for h in range(2):
                side(w, t, h).wait_send()
            gather_x(w, t).wait_send()
            relay(w, t).wait_send()
        to_near(w).wait_send()
        to_far(w).wait_send()
        gather_far(w, False).wait_send()
        gather_near(w, False).wait_send()
    for w in range(WAVES):
        for xx in range(4):
            for t in range(2):
                store(w, xx, t).wait()


def shards(observed, mask, basis, coeffs, lag_set, ar_weight):
    vm = pltpu.VMEM
    dma = pltpu.SemaphoreType.DMA
    scratch = [
        vm((ROWS, COLS), BF),
        vm((32, ROWS), jnp.int32),
        vm((ROWS, COLS), BF),
        vm((COLS, R), BF),
        vm((2, 4, 2, 2, OWN, R), BF),
        vm((4, 256, R), F32),
        vm((4, 128, R), BF),
        vm((4, 128, R), BF),
        vm((4, 128, R), BF),
        vm((4, 128, R), BF),
        vm((128, R), BF),
        vm((128, R), BF),
        vm((128, R), F32),
        vm((128, R), F32),
        vm((OWN, R), F32),
        vm((ROWS + 72, R), F32),
        vm((2, 32, R), BF),
        vm((ROWS + 40, R), F32),
        vm((3, 8, R), F32),
        vm((ROWS, R), F32),
        vm((ROWS, R), BF),
        vm((4, 1, 128), F32),
        vm((4, 1, 128), F32),
        vm((2, 1, 128), F32),
        vm((R, ROWS), BF),
        vm((WAVES, 2, 128, WV), F32),
        vm((WAVES, R, WV), F32),
        vm((WAVES, R, WV), BF),
        vm((WAVES, R, WV), BF),
        vm((WAVES, 2, R, WV), BF),
        vm((WAVES, 2, R, WV), BF),
        vm((WAVES, R, SUB), BF),
        vm((WAVES, R, SUB), BF),
        vm((WAVES, SUB, SUB), BF),
        vm((WAVES, SUB, SUB), BF),
        vm((2, COLS, 128), BF),
        dma((3,)),
        dma((2,)), dma((2,)), dma((2, 4)), dma((2, 4)), dma((2, 4)), dma((2, 4)),
        dma((2,)), dma((2,)), dma((2,)), dma((2,)),
        dma((4,)), dma((4,)), dma((4,)), dma((4,)), dma, dma,
        dma((2,)), dma((2,)),
        dma((WAVES, 2)), dma((WAVES, 2)), dma((WAVES, 2, 2)), dma((WAVES, 2, 2)),
        dma((WAVES, 2)), dma((WAVES, 2)), dma((WAVES, 2)), dma((WAVES, 2)),
        dma((WAVES, 2)), dma((WAVES, 2)), dma((WAVES, 2)), dma((WAVES, 2)),
        dma((WAVES, 4, 2)),
    ]
    anyspace = pl.BlockSpec(memory_space=pl.ANY)
    vmem = pl.BlockSpec(memory_space=pltpu.VMEM)
    return pl.pallas_call(
        kernel,
        out_shape=(
            jax.ShapeDtypeStruct((OWN, R), F32),
            jax.ShapeDtypeStruct((COLS, R), BF),
        ),
        in_specs=[anyspace, anyspace, anyspace, vmem, pl.BlockSpec(memory_space=pltpu.SMEM), vmem],
        out_specs=(vmem, anyspace),
        scratch_shapes=scratch,
        compiler_params=pltpu.CompilerParams(
            collective_id=0, has_side_effects=True, vmem_limit_bytes=60 * 2**20
        ),
        name="alternation",
    )(observed, mask.T, basis, coeffs, lag_set, ar_weight)


def solution(mesh):
    placed = (
        P("frames", "verts"),
        P("frames", "verts"),
        P("verts", None),
        P(("frames", "verts"), None),
        P(),
        P(),
    )
    return jax.shard_map(
        shards,
        mesh=mesh,
        in_specs=placed,
        out_specs=(P(("frames", "verts"), None), P("verts", None)),
        check_vma=False,
    )
```

```python
import jax
import jax.numpy as jnp
from jax import lax
from jax.experimental import pallas as pl
from jax.experimental.pallas import tpu as pltpu
from jax.sharding import PartitionSpec as P

R = 256
NLAG = 8
LAGMAX = 32
GRP = 128
ROWS = 1024
COLS = 4096
OWN = 64
NF = 16384
BF = jnp.bfloat16
F32 = jnp.float32
MESH = pl.DeviceIdType.MESH
NT = (((1,), (1,)), ((), ()))
WAVES = 4
WV = 256
SUB = 128


def kernel(
    obs_hbm, maskt_hbm, basis_hbm, coeff_ref, lag_ref, arw_ref,
    newc_ref, newb_hbm,
    obs, mt, mexp, basis, ag, dacc, rs_s, rs_r, ry_s, ry_r, rz_s, rz_r, zpart,
    xe, px, gfull, ghalo, rbuf, sums, pgb, cn, stat1, stat2, mine,
    ct, gacc, gown, s_opp, r_opp, s_side, r_side, s_z, r_z, nb,
    ld_sem, ag_zs, ag_zr, ag_ys, ag_yr, ag_cs, ag_cr,
    halo_s, halo_r, gh_s, gh_r, rc_ss, rc_rs, ry_ss, ry_rs, rz_ss, rz_rs,
    st_s, st_r, opp_s, opp_rs, side_s, side_rs, z_s, z_rs,
    az_s, az_r, ax_s, ax_r, rel_s, rel_r, out_sem,
):
    f = lax.axis_index("frames")
    v = lax.axis_index("verts")
    y, z, c = v // 4, (v // 2) % 2, v % 2
    zl, x = f // 4, f % 4
    glob = f * 16 + v
    has_prev = glob > 0
    has_next = glob < 255
    prev_dev = ((glob + 255) % 256 // 16, (glob + 255) % 16)
    next_dev = ((glob + 1) % 256 // 16, (glob + 1) % 16)

    below = ((f + 15) % 16, v)
    above = ((f + 1) % 16, v)

    def vdev(yy, zz, cc):
        return (f, yy * 4 + zz * 2 + cc)

    def fdev(zz, xx):
        return (zz * 4 + xx, v)

    sib = vdev(y, z, 1 - c)
    zpeer = vdev(y, 1 - z, c)
    right = fdev(zl, (x + 1) % 4)
    left = fdev(zl, (x + 3) % 4)

    def remote(src, dst, ssem, rsem, dev):
        return pltpu.make_async_remote_copy(
            src_ref=src, dst_ref=dst, send_sem=ssem, recv_sem=rsem,
            device_id=dev, device_id_type=MESH,
        )

    def load_obs(yy, cc, zz):
        return pltpu.make_async_copy(
            obs_hbm.at[pl.ds(yy * 256 + zz * 128 + cc * 64, 64)],
            obs.at[pl.ds(yy * 256 + cc * 128 + zz * 64, 64)],
            ld_sem.at[0],
        )

    def load_basis():
        return pltpu.make_async_copy(basis_hbm, basis, ld_sem.at[1])

    def load_mask():
        return pltpu.make_async_copy(maskt_hbm, mt, ld_sem.at[2])

    load_mask().start()
    load_basis().start()
    for yy in range(4):
        for cc in range(2):
            for zz in range(2):
                load_obs(yy, cc, zz).start()

    barrier = pltpu.get_barrier_semaphore()

    for d in range(1, 4):
        for dev in (vdev((y + d) % 4, z, c), fdev(zl, (x + d) % 4), fdev((zl + d) % 4, x)):
            pl.semaphore_signal(barrier, inc=1, device_id=dev, device_id_type=MESH)
    for dev in (zpeer, sib):
        pl.semaphore_signal(barrier, inc=1, device_id=dev, device_id_type=MESH)
    for has, dev in (
        (has_prev, prev_dev), (has_next, next_dev), (f > 0, below), (f < 15, above)
    ):

        @pl.when(has)
        def _():
            pl.semaphore_signal(barrier, inc=1, device_id=dev, device_id_type=MESH)

    own = coeff_ref[...]
    ag[0, y, c, z] = (own.astype(BF) * 0.0625).astype(BF)
    xe[32:96] = own

    @pl.when(glob == 0)
    def _():
        xe[0:32] = jnp.zeros((32, R), F32)

    @pl.when(glob == 255)
    def _():
        xe[96:128] = jnp.zeros((32, R), F32)

    @pl.when(f == 0)
    def _():
        ghalo[0] = jnp.zeros((32, R), BF)

    @pl.when(f == 15)
    def _():
        ghalo[1] = jnp.zeros((32, R), BF)

    def expand(k):
        yy = (y + 4 - k) % 4
        for zz in range(2):
            src = pl.multiple_of(yy * 256 + zz * 128, 128)
            m = mt[:, pl.ds(src, 128)].astype(F32).T
            for cc in range(2):
                dst = pl.multiple_of(yy * 256 + cc * 128 + zz * 64, 64)
                for g in range(32):
                    mexp[pl.ds(dst, 64), g * 128 : (g + 1) * 128] = jnp.broadcast_to(
                        m[cc * 64 : cc * 64 + 64, g : g + 1], (64, 128)
                    ).astype(BF)

    load_mask().wait()
    pl.loop(0, 2)(expand)
    pl.semaphore_wait(
        barrier,
        11 + has_prev.astype(jnp.int32) + has_next.astype(jnp.int32)
        + (f > 0).astype(jnp.int32) + (f < 15).astype(jnp.int32),
    )

    def ag_z(i):
        return remote(ag.at[i, y, c, z], ag.at[i, y, c, z], ag_zs.at[i], ag_zr.at[i], zpeer)

    def ag_y(i, d):
        return remote(
            ag.at[i, y, c], ag.at[i, y, c], ag_ys.at[i, d], ag_yr.at[i, d],
            vdev((y + d) % 4, z, c),
        )

    def ag_y_got(i, d):
        s = (y + 4 - d) % 4
        return remote(ag.at[i, s, c], ag.at[i, s, c], ag_ys.at[i, d], ag_yr.at[i, d], sib)

    def ag_c(i, d):
        s = (y + 4 - d) % 4
        return remote(ag.at[i, s, c], ag.at[i, s, c], ag_cs.at[i, d], ag_cr.at[i, d], sib)

    def halo(up):
        if up:
            return remote(
                xe.at[pl.ds(64, 32)], xe.at[pl.ds(0, 32)], halo_s.at[0], halo_r.at[0], next_dev
            )
        return remote(
            xe.at[pl.ds(32, 32)], xe.at[pl.ds(96, 32)], halo_s.at[1], halo_r.at[1], prev_dev
        )

    def ghalo_copy(up):
        if up:
            return remote(
                ag.at[1, 3, 1, 1, pl.ds(32, 32)], ghalo.at[0], gh_s.at[0], gh_r.at[0], above
            )
        return remote(ag.at[1, 0, 0, 0, pl.ds(0, 32)], ghalo.at[1], gh_s.at[1], gh_r.at[1], below)

    def ends(copy, lower, upper, act):
        @pl.when(upper)
        def _():
            d = copy(act != "recv")
            d.start() if act == "start" else d.wait_recv() if act == "recv" else d.wait_send()

        @pl.when(lower)
        def _():
            d = copy(act == "recv")
            d.start() if act == "start" else d.wait_recv() if act == "recv" else d.wait_send()

    def prior(window, n, first):
        m = n + 32
        r = window[32:]
        for l in range(NLAG):
            r = r - arw_ref[l : l + 1, :] * pltpu.roll(window, lag_ref[l], 0)[32:]
        frame = first + lax.broadcasted_iota(jnp.int32, (m, R), 0)
        r = jnp.where((frame >= LAGMAX) & (frame < NF), r, 0.0)
        grad = r[0:n]
        for l in range(NLAG):
            grad = grad - arw_ref[l : l + 1, :] * pltpu.roll(r, m - lag_ref[l], 0)[0:n]
        return grad

    ag_z(0).start()
    ends(halo, has_prev, has_next, "start")
    ag_z(0).wait_recv()
    for d in range(1, 4):
        ag_y(0, d).start()
    ag_c(0, 0).start()
    pl.loop(2, 4)(expand)
    ends(halo, has_prev, has_next, "recv")
    px[...] = prior(xe[...], OWN, glob * OWN)
    load_basis().wait()
    pltpu.make_async_copy(obs_hbm, obs, ld_sem.at[0]).wait()

    def rs_core(k):
        return remote(rs_s.at[k], rs_r.at[k], rc_ss.at[k], rc_rs.at[k], sib)

    def rs_y(k):
        return remote(
            ry_s.at[k], ry_r.at[k], ry_ss.at[k], ry_rs.at[k], vdev((y + 4 - k) % 4, z, c)
        )

    @pl.loop(0, 4)
    def _(k):
        ag_c(0, k).wait_recv()
        yy = (y + 4 - k) % 4
        base = pl.multiple_of(yy * 256, 256)
        low = ag[0, yy].reshape(256, R)
        dacc[k] = jnp.zeros((256, R), F32)

        @pl.loop(0, 2)
        def _(jj):
            for u in range(2):
                cols = pl.ds(pl.multiple_of((jj * 2 + u) * 1024, 1024), 1024)
                b = basis[cols, :]
                prod = lax.dot_general(low, b, NT, preferred_element_type=F32)
                e = (prod - obs[pl.ds(base, 256), cols].astype(F32)).astype(BF) * mexp[
                    pl.ds(base, 256), cols
                ]
                dacc[k] += jnp.dot(e, b, preferred_element_type=F32)

        rs_s[k] = dacc[k, pl.ds(pl.multiple_of((1 - c) * 128, 128), 128), :].astype(BF)
        rs_core(k).start()

        @pl.when(k == 0)
        def _():
            for d in range(1, 4):
                ag_y_got(0, d).wait_recv()
                ag_c(0, d).start()

        @pl.when(k >= 2)
        def _():
            rs_core(k - 1).wait_recv()
            ry_s[k - 1] = (
                dacc[k - 1, pl.ds(pl.multiple_of(c * 128, 128), 128), :]
                + rs_r[k - 1].astype(F32)
            ).astype(BF)
            rs_y(k - 1).start()

    rs_core(3).wait_recv()
    ry_s[3] = (
        dacc[3, pl.ds(pl.multiple_of(c * 128, 128), 128), :] + rs_r[3].astype(F32)
    ).astype(BF)
    rs_y(3).start()
    rs_core(0).wait_recv()
    part = dacc[0, pl.ds(pl.multiple_of(c * 128, 128), 128), :] + rs_r[0].astype(F32)
    for k in range(1, 4):
        rs_y(k).wait_recv()
        part = part + ry_r[k].astype(F32)
    zpart[...] = part * (2.0 ** -12)
    mine_rows = pl.ds(pl.multiple_of(z * 64, 64), 64)
    zpart[mine_rows, :] += px[...]
    rz_s[...] = zpart[...].astype(BF)
    rs_z = remote(rz_s, rz_r, rz_ss, rz_rs, zpeer)
    rs_z.start()
    rs_z.wait_recv()

    g128 = zpart[...] + rz_r[...].astype(F32)
    zpart[...] = g128
    ag[1, y, c] = g128.astype(BF).reshape(2, OWN, R)
    for d in range(1, 4):
        ag_y(1, d).start()
    ag_c(1, 0).start()
    for d in range(1, 4):
        ag_y_got(1, d).wait_recv()
        ag_c(1, d).start()
    for k in range(4):
        ag_c(1, k).wait_recv()
    ends(ghalo_copy, f > 0, f < 15, "start")
    def blocks(act):
        @pl.loop(0, 4)
        def _(yy):
            for cc in range(2):
                for zz in range(2):
                    frame = pl.multiple_of(yy * 256 + zz * 128 + cc * 64, 64)
                    place = pl.multiple_of(yy * 256 + cc * 128 + zz * 64, 64)
                    act(yy, cc, zz, frame, place)

    def widen(yy, cc, zz, frame, place):
        gfull[pl.ds(40 + frame, OWN), :] = ag[1, yy, cc, zz].astype(F32)

    blocks(widen)
    sub8 = lax.broadcasted_iota(jnp.int32, (1, 8, R), 1)

    def moved(turned, tiles):
        n = turned.shape[0] - 4
        a = jnp.where((tiles & 1) == 1, turned[1:], turned[:-1])
        a = jnp.where((tiles & 2) == 2, a[2:], a[:-2])
        return jnp.where(tiles == 4, turned[4:], a[:n]).reshape(n * 8, R)

    def earlier(window, lag):
        low = lag & 7
        turned = pltpu.roll(window, low, 1)
        near_rows = jnp.where(sub8 >= low, turned[1:], turned[:-1])
        return moved(near_rows, 4 - ((sub8 * 0 + lag) >> 3))

    def later(window, lag):
        low = lag & 7
        turned = pltpu.roll(window, (8 - low) & 7, 1)
        near_rows = jnp.where(sub8 < 8 - low, turned[:-1], turned[1:])
        return moved(near_rows, (sub8 * 0 + lag) >> 3)

    gfull[0:8] = jnp.zeros((8, R), F32)
    rbuf[1056:1064] = jnp.zeros((8, R), F32)

    @pl.loop(0, 11)
    def _(i):
        @pl.when(i == 9)
        def _():
            ends(ghalo_copy, f > 0, f < 15, "recv")
            gfull[8:40] = ghalo[0].astype(F32)
            gfull[1064:1096] = ghalo[1].astype(F32)

        at = pl.multiple_of((i + 1) % 11 * 96, 8)
        window = gfull[pl.ds(at, 136), :].reshape(17, 8, R)
        r = gfull[pl.ds(40 + at, 96), :]
        for l in range(NLAG):
            r = r - arw_ref[l : l + 1, :] * earlier(window, lag_ref[l])
        frame = f * ROWS + at + lax.broadcasted_iota(jnp.int32, (96, R), 0)
        rbuf[pl.ds(at, 96), :] = jnp.where((frame >= LAGMAX) & (frame < NF), r, 0.0)

    sums[...] = jnp.zeros_like(sums)

    @pl.loop(0, 8)
    def _(i):
        at = pl.multiple_of(i * 128, 128)
        window = rbuf[pl.ds(at, 168), :].reshape(21, 8, R)
        p = rbuf[pl.ds(at, 128), :]
        for l in range(NLAG):
            p = p - arw_ref[l : l + 1, :] * later(window, lag_ref[l])
        pgb[pl.ds(at, 128), :] = p
        g = gfull[pl.ds(40 + at, 128), :]
        for n, val in enumerate((g * g, g * p, p * p)):
            sums[n] += jnp.sum(val.reshape(16, 8, R), axis=0)

    lane = lax.broadcasted_iota(jnp.int32, (1, 128), 1)
    s1, s12, s2 = [
        jnp.sum(jnp.sum(sums[n], axis=0, keepdims=True), axis=1, keepdims=True) for n in range(3)
    ]
    row = jnp.where(
        lane == 0, s1, jnp.where(lane == 1, s12, jnp.where(lane == 2, s2, 0.0))
    )

    def exchange(val, slots, i, at, dev_of):
        mine[i] = val
        slots[at] = val
        for d in range(1, 4):
            remote(mine.at[i], slots.at[at], st_s.at[i], st_r.at[i], dev_of(d)).start()

        def whole():
            return remote(slots.at[pl.ds(0, 3)], slots.at[pl.ds(0, 3)], st_s.at[i], st_r.at[i], sib)

        whole().wait_recv()
        whole().wait_send()
        return jnp.sum(slots[...], axis=0)

    row = exchange(row, stat1, 0, x, lambda d: fdev(zl, (x + d) % 4))
    row = exchange(row, stat2, 1, zl, lambda d: fdev((zl + d) % 4, x))

    def pick(i):
        return jnp.sum(jnp.where(lane == i, row, 0.0), axis=1, keepdims=True)

    inv = 1.0 / (NF * R)
    ss1, s12, s22 = pick(0), pick(1), pick(2)
    b1 = 0.3 / jnp.sqrt(ss1 * inv + 1e-6)
    ss2 = jnp.maximum(ss1 - 2.0 * b1 * s12 + b1 * b1 * s22, 0.0)
    b2 = 0.3 / jnp.sqrt(ss2 * inv + 1e-6)
    by_g, by_p = b1 + b2, b1 * b2
    def step(yy, cc, zz, frame, place):
        low = ag[0, yy, cc, zz].astype(F32) - 0.0625 * (
            by_g * gfull[pl.ds(40 + frame, OWN), :] - by_p * pgb[pl.ds(frame, OWN), :]
        )
        cn[pl.ds(place, OWN), :] = low.astype(BF)

    blocks(step)

    @pl.loop(0, 4)
    def _(yy):
        at = pl.multiple_of(yy * 256, 256)
        ct[:, pl.ds(at, 256)] = cn[pl.ds(at, 256), :].T

    own_at = pl.multiple_of(v * OWN, OWN)
    newc_ref[...] = (
        coeff_ref[...] - by_g * zpart[mine_rows, :] + by_p * pgb[pl.ds(own_at, OWN), :]
    )

    def opp(w, s):
        half = pl.ds(s * 128, 128)
        return remote(
            s_opp.at[w, half], r_opp.at[w, half], opp_s.at[w, s], opp_rs.at[w, s],
            right if s == 0 else left,
        )

    def side(w, d, h):
        half = pl.ds(h * 128, 128)
        return remote(
            s_side.at[w, d, half], r_side.at[w, d, half],
            side_s.at[w, d, h], side_rs.at[w, d, h], right if d == 0 else left,
        )

    def two_blocks(w, xa, xb):
        def both(ref):
            return jnp.concatenate(
                [ref[:, pl.ds(pl.multiple_of(t * 1024 + w * WV, WV), WV)] for t in (xa, xb)], axis=1
            )

        b = jnp.concatenate(
            [basis[pl.ds(pl.multiple_of(t * 1024 + w * WV, WV), WV), :] for t in (xa, xb)], axis=0
        )
        prod = lax.dot_general(cn[...], b, NT, preferred_element_type=F32)
        e = (prod - both(obs).astype(F32)).astype(BF) * both(mexp)
        return jnp.dot(ct[...], e, preferred_element_type=F32)

    def compute(w):
        g = two_blocks(w, (x + 2) % 4, (x + 1) % 4)
        s_opp[w] = g[:, 0:WV].astype(BF)
        opp(w, 0).start()
        opp(w, 1).start()
        s_side[w, 0, 128:256] = g[128:256, WV:].astype(BF)
        side(w, 0, 1).start()
        gacc[w, 0] = g[0:128, WV:]
        g = two_blocks(w, (x + 3) % 4, x)
        s_side[w, 1, 0:128] = g[0:128, 0:WV].astype(BF)
        side(w, 1, 0).start()
        gacc[w, 1] = g[128:256, 0:WV]
        gown[w] = g[:, WV:]

    def join(w):
        opp(w, 0).wait_recv()
        s_side[w, 0, 0:128] = (gacc[w, 0] + r_opp[w, 0:128].astype(F32)).astype(BF)
        side(w, 0, 0).start()
        opp(w, 1).wait_recv()
        s_side[w, 1, 128:256] = (gacc[w, 1] + r_opp[w, 128:256].astype(F32)).astype(BF)
        side(w, 1, 1).start()

    def zsum(w, d):
        return remote(
            s_z.at[w, d], r_z.at[w, d], z_s.at[w, d], z_rs.at[w, d], fdev((zl + d) % 4, x)
        )

    def quarter(s):
        return (
            pl.ds(pl.multiple_of(s // 2 * SUB, SUB), SUB),
            pl.ds(pl.multiple_of(s % 2 * SUB, SUB), SUB),
        )

    def reduce_x(w):
        for d in range(2):
            for h in range(2):
                side(w, d, h).wait_recv()
        gown[w] = gown[w] + r_side[w, 0].astype(F32) + r_side[w, 1].astype(F32)
        for d in (2, 1, 3):
            ranks, verts = quarter((zl + d) % 4)
            s_z[w, d] = gown[w, ranks, verts].astype(BF)
            zsum(w, d).start()

    def quarter_of(w, s):
        return nb.at[s // 2, pl.ds(pl.multiple_of(x * 1024 + w * WV + s % 2 * SUB, SUB), SUB)]

    def block_of(w, xx):
        return nb.at[:, pl.ds(pl.multiple_of(xx * 1024 + w * WV, WV), WV)]

    def half_of(w, xx, t):
        return nb.at[t, pl.ds(pl.multiple_of(xx * 1024 + w * WV, WV), WV)]

    def gather_z(w, d):
        part = quarter_of(w, zl)
        return remote(part, part, az_s.at[w, d], az_r.at[w, d], fdev((zl + d) % 4, x))

    def gather_z_got(w, d):
        part = quarter_of(w, (zl + 4 - d) % 4)
        return remote(part, part, az_s.at[w, d], az_r.at[w, d], left)

    def gather_x(w, t):
        part = block_of(w, x)
        return remote(part, part, ax_s.at[w, t], ax_r.at[w, t], right if t == 0 else left)

    def gather_x_got(w, t):
        part = block_of(w, (x + (3 if t == 0 else 1)) % 4)
        return remote(part, part, ax_s.at[w, t], ax_r.at[w, t], left)

    def relay(w, t):
        part = half_of(w, (x + (3 if t == 0 else 1)) % 4, t)
        return remote(part, part, rel_s.at[w, t], rel_r.at[w, t], right if t == 0 else left)

    def relay_got(w, t):
        part = half_of(w, (x + 2) % 4, t)
        return remote(part, part, rel_s.at[w, t], rel_r.at[w, t], left)

    def store(w, xx, t):
        rows = pl.ds(xx * 1024 + w * WV, WV)
        return pltpu.make_async_copy(
            nb.at[t, rows], newb_hbm.at[rows, pl.ds(t * 128, 128)], out_sem.at[w, xx, t]
        )

    def update(w):
        ranks, verts = quarter(zl)
        acc = gown[w, ranks, verts]
        for d in range(1, 4):
            zsum(w, d).wait_recv()
            acc = acc + r_z[w, d].astype(F32)
        rows = pl.ds(pl.multiple_of(x * 1024 + w * WV + zl % 2 * SUB, SUB), SUB)
        nb[zl // 2, rows, :] = (
            basis[rows, ranks].astype(F32) - (2.0 ** -6) * acc.T
        ).astype(BF)
        for d in (2, 1, 3):
            gather_z(w, d).start()

    def spread(w):
        for d in range(1, 4):
            gather_z_got(w, d).wait_recv()
        gather_x(w, 0).start()
        gather_x(w, 1).start()

    def pass_on(w):
        for t in range(2):
            gather_x_got(w, t).wait_recv()
            relay(w, t).start()

    def finish(w):
        for t in range(2):
            relay_got(w, t).wait_recv()
        for xx in range(4):
            for t in range(2):
                store(w, xx, t).start()

    for act, w in (
        (compute, 0), (compute, 1), (join, 0), (compute, 2), (join, 1), (reduce_x, 0),
        (compute, 3), (join, 2), (update, 0), (reduce_x, 1), (join, 3), (spread, 0),
        (update, 1), (reduce_x, 2), (spread, 1), (reduce_x, 3), (update, 2), (pass_on, 0),
        (update, 3), (spread, 2), (pass_on, 1), (spread, 3), (finish, 0), (pass_on, 2),
        (finish, 1), (pass_on, 3), (finish, 2), (finish, 3),
    ):
        act(w)

    ag_z(0).wait_send()
    for i in range(2):
        for d in range(1, 4):
            ag_y(i, d).wait_send()
        for d in range(4):
            ag_c(i, d).wait_send()
    ends(halo, has_prev, has_next, "send")
    ends(ghalo_copy, f > 0, f < 15, "send")
    for k in range(4):
        rs_core(k).wait_send()
        if k:
            rs_y(k).wait_send()
    rs_z.wait_send()
    for w in range(WAVES):
        for t in range(2):
            opp(w, t).wait_send()
            for h in range(2):
                side(w, t, h).wait_send()
            gather_x(w, t).wait_send()
            relay(w, t).wait_send()
        for d in range(1, 4):
            zsum(w, d).wait_send()
            gather_z(w, d).wait_send()
    for w in range(WAVES):
        for xx in range(4):
            for t in range(2):
                store(w, xx, t).wait()


def shards(observed, mask, basis, coeffs, lag_set, ar_weight):
    vm = pltpu.VMEM
    dma = pltpu.SemaphoreType.DMA
    scratch = [
        vm((ROWS, COLS), BF),
        vm((32, ROWS), jnp.int32),
        vm((ROWS, COLS), BF),
        vm((COLS, R), BF),
        vm((2, 4, 2, 2, OWN, R), BF),
        vm((4, 256, R), F32),
        vm((4, 128, R), BF),
        vm((4, 128, R), BF),
        vm((4, 128, R), BF),
        vm((4, 128, R), BF),
        vm((128, R), BF),
        vm((128, R), BF),
        vm((128, R), F32),
        vm((128, R), F32),
        vm((OWN, R), F32),
        vm((ROWS + 72, R), F32),
        vm((2, 32, R), BF),
        vm((ROWS + 40, R), F32),
        vm((3, 8, R), F32),
        vm((ROWS, R), F32),
        vm((ROWS, R), BF),
        vm((4, 1, 128), F32),
        vm((4, 1, 128), F32),
        vm((2, 1, 128), F32),
        vm((R, ROWS), BF),
        vm((WAVES, 2, 128, WV), F32),
        vm((WAVES, R, WV), F32),
        vm((WAVES, R, WV), BF),
        vm((WAVES, R, WV), BF),
        vm((WAVES, 2, R, WV), BF),
        vm((WAVES, 2, R, WV), BF),
        vm((WAVES, 4, SUB, SUB), BF),
        vm((WAVES, 4, SUB, SUB), BF),
        vm((2, COLS, 128), BF),
        dma((3,)),
        dma((2,)), dma((2,)), dma((2, 4)), dma((2, 4)), dma((2, 4)), dma((2, 4)),
        dma((2,)), dma((2,)), dma((2,)), dma((2,)),
        dma((4,)), dma((4,)), dma((4,)), dma((4,)), dma, dma,
        dma((2,)), dma((2,)),
        dma((WAVES, 2)), dma((WAVES, 2)), dma((WAVES, 2, 2)), dma((WAVES, 2, 2)),
        dma((WAVES, 4)), dma((WAVES, 4)), dma((WAVES, 4)), dma((WAVES, 4)),
        dma((WAVES, 2)), dma((WAVES, 2)), dma((WAVES, 2)), dma((WAVES, 2)),
        dma((WAVES, 4, 2)),
    ]
    anyspace = pl.BlockSpec(memory_space=pl.ANY)
    vmem = pl.BlockSpec(memory_space=pltpu.VMEM)
    return pl.pallas_call(
        kernel,
        out_shape=(
            jax.ShapeDtypeStruct((OWN, R), F32),
            jax.ShapeDtypeStruct((COLS, R), BF),
        ),
        in_specs=[anyspace, anyspace, anyspace, vmem, pl.BlockSpec(memory_space=pltpu.SMEM), vmem],
        out_specs=(vmem, anyspace),
        scratch_shapes=scratch,
        compiler_params=pltpu.CompilerParams(
            collective_id=0, has_side_effects=True, vmem_limit_bytes=60 * 2**20
        ),
        name="alternation",
    )(observed, mask.T, basis, coeffs, lag_set, ar_weight)


def solution(mesh):
    placed = (
        P("frames", "verts"),
        P("frames", "verts"),
        P("verts", None),
        P(("frames", "verts"), None),
        P(),
        P(),
    )
    return jax.shard_map(
        shards,
        mesh=mesh,
        in_specs=placed,
        out_specs=(P(("frames", "verts"), None), P("verts", None)),
        check_vma=False,
    )
```

```python
import jax
import jax.numpy as jnp
from jax import lax
from jax.experimental import pallas as pl
from jax.experimental.pallas import tpu as pltpu
from jax.sharding import PartitionSpec as P

R = 256
NLAG = 8
LAGMAX = 32
GRP = 128
ROWS = 1024
COLS = 4096
OWN = 64
NF = 16384
BF = jnp.bfloat16
F32 = jnp.float32
MESH = pl.DeviceIdType.MESH
NT = (((1,), (1,)), ((), ()))
WAVES = 4
WV = 256
SUB = 128


def kernel(
    obs_hbm, maskt_hbm, basis_hbm, coeff_ref, lag_ref, arw_ref,
    newc_ref, newb_hbm,
    obs, mt, mexp, basis, ag, dacc, rs_s, rs_r, ry_s, ry_r, rz_s, rz_r, zpart,
    xe, px, gfull, ghalo, rbuf, sums, pgb, cn, stat1, stat2, mine,
    ct, gacc, gown, s_opp, r_opp, s_side, r_side, s_z, r_z, nb,
    ld_sem, ag_zs, ag_zr, ag_ys, ag_yr, ag_cs, ag_cr,
    halo_s, halo_r, gh_s, gh_r, rc_ss, rc_rs, ry_ss, ry_rs, rz_ss, rz_rs,
    st_s, st_r, opp_s, opp_rs, side_s, side_rs, z_s, z_rs,
    az_s, az_r, ax_s, ax_r, rel_s, rel_r, out_sem,
):
    f = lax.axis_index("frames")
    v = lax.axis_index("verts")
    y, z, c = v // 4, (v // 2) % 2, v % 2
    zl, x = f // 4, f % 4
    glob = f * 16 + v
    has_prev = glob > 0
    has_next = glob < 255
    prev_dev = ((glob + 255) % 256 // 16, (glob + 255) % 16)
    next_dev = ((glob + 1) % 256 // 16, (glob + 1) % 16)

    below = ((f + 15) % 16, v)
    above = ((f + 1) % 16, v)

    def vdev(yy, zz, cc):
        return (f, yy * 4 + zz * 2 + cc)

    def fdev(zz, xx):
        return (zz * 4 + xx, v)

    sib = vdev(y, z, 1 - c)
    zpeer = vdev(y, 1 - z, c)
    right = fdev(zl, (x + 1) % 4)
    left = fdev(zl, (x + 3) % 4)

    def remote(src, dst, ssem, rsem, dev):
        return pltpu.make_async_remote_copy(
            src_ref=src, dst_ref=dst, send_sem=ssem, recv_sem=rsem,
            device_id=dev, device_id_type=MESH,
        )

    def load_obs(yy, cc, zz):
        return pltpu.make_async_copy(
            obs_hbm.at[pl.ds(yy * 256 + zz * 128 + cc * 64, 64)],
            obs.at[pl.ds(yy * 256 + cc * 128 + zz * 64, 64)],
            ld_sem.at[0],
        )

    def load_basis():
        return pltpu.make_async_copy(basis_hbm, basis, ld_sem.at[1])

    def load_mask():
        return pltpu.make_async_copy(maskt_hbm, mt, ld_sem.at[2])

    load_mask().start()
    load_basis().start()
    for yy in range(4):
        for cc in range(2):
            for zz in range(2):
                load_obs(yy, cc, zz).start()

    barrier = pltpu.get_barrier_semaphore()

    for d in range(1, 4):
        for dev in (vdev((y + d) % 4, z, c), fdev(zl, (x + d) % 4), fdev((zl + d) % 4, x)):
            pl.semaphore_signal(barrier, inc=1, device_id=dev, device_id_type=MESH)
    for dev in (zpeer, sib):
        pl.semaphore_signal(barrier, inc=1, device_id=dev, device_id_type=MESH)
    for has, dev in (
        (has_prev, prev_dev), (has_next, next_dev), (f > 0, below), (f < 15, above)
    ):

        @pl.when(has)
        def _():
            pl.semaphore_signal(barrier, inc=1, device_id=dev, device_id_type=MESH)

    own = coeff_ref[...]
    ag[0, y, c, z] = (own.astype(BF) * 0.0625).astype(BF)
    xe[32:96] = own

    @pl.when(glob == 0)
    def _():
        xe[0:32] = jnp.zeros((32, R), F32)

    @pl.when(glob == 255)
    def _():
        xe[96:128] = jnp.zeros((32, R), F32)

    @pl.when(f == 0)
    def _():
        ghalo[0] = jnp.zeros((32, R), BF)

    @pl.when(f == 15)
    def _():
        ghalo[1] = jnp.zeros((32, R), BF)

    def expand(k):
        yy = (y + 4 - k) % 4
        for zz in range(2):
            src = pl.multiple_of(yy * 256 + zz * 128, 128)
            m = mt[:, pl.ds(src, 128)].astype(F32).T
            for cc in range(2):
                dst = pl.multiple_of(yy * 256 + cc * 128 + zz * 64, 64)
                for g in range(32):
                    mexp[pl.ds(dst, 64), g * 128 : (g + 1) * 128] = jnp.broadcast_to(
                        m[cc * 64 : cc * 64 + 64, g : g + 1], (64, 128)
                    ).astype(BF)

    pl.semaphore_wait(
        barrier,
        11 + has_prev.astype(jnp.int32) + has_next.astype(jnp.int32)
        + (f > 0).astype(jnp.int32) + (f < 15).astype(jnp.int32),
    )

    def ag_z(i):
        return remote(ag.at[i, y, c, z], ag.at[i, y, c, z], ag_zs.at[i], ag_zr.at[i], zpeer)

    def ag_y(i, d):
        return remote(
            ag.at[i, y, c], ag.at[i, y, c], ag_ys.at[i, d], ag_yr.at[i, d],
            vdev((y + d) % 4, z, c),
        )

    def ag_y_got(i, d):
        s = (y + 4 - d) % 4
        return remote(ag.at[i, s, c], ag.at[i, s, c], ag_ys.at[i, d], ag_yr.at[i, d], sib)

    def ag_c(i, d):
        s = (y + 4 - d) % 4
        return remote(ag.at[i, s, c], ag.at[i, s, c], ag_cs.at[i, d], ag_cr.at[i, d], sib)

    def halo(up):
        if up:
            return remote(
                xe.at[pl.ds(64, 32)], xe.at[pl.ds(0, 32)], halo_s.at[0], halo_r.at[0], next_dev
            )
        return remote(
            xe.at[pl.ds(32, 32)], xe.at[pl.ds(96, 32)], halo_s.at[1], halo_r.at[1], prev_dev
        )

    def ghalo_copy(up):
        if up:
            return remote(
                ag.at[1, 3, 1, 1, pl.ds(32, 32)], ghalo.at[0], gh_s.at[0], gh_r.at[0], above
            )
        return remote(ag.at[1, 0, 0, 0, pl.ds(0, 32)], ghalo.at[1], gh_s.at[1], gh_r.at[1], below)

    def ends(copy, lower, upper, act):
        @pl.when(upper)
        def _():
            d = copy(act != "recv")
            d.start() if act == "start" else d.wait_recv() if act == "recv" else d.wait_send()

        @pl.when(lower)
        def _():
            d = copy(act == "recv")
            d.start() if act == "start" else d.wait_recv() if act == "recv" else d.wait_send()

    def prior(window, n, first):
        m = n + 32
        r = window[32:]
        for l in range(NLAG):
            r = r - arw_ref[l : l + 1, :] * pltpu.roll(window, lag_ref[l], 0)[32:]
        frame = first + lax.broadcasted_iota(jnp.int32, (m, R), 0)
        r = jnp.where((frame >= LAGMAX) & (frame < NF), r, 0.0)
        grad = r[0:n]
        for l in range(NLAG):
            grad = grad - arw_ref[l : l + 1, :] * pltpu.roll(r, m - lag_ref[l], 0)[0:n]
        return grad

    ag_z(0).start()
    ends(halo, has_prev, has_next, "start")
    load_mask().wait()
    pl.loop(0, 2)(expand)
    ag_z(0).wait_recv()
    for d in range(1, 4):
        ag_y(0, d).start()
    ag_c(0, 0).start()
    expand(2)
    ends(halo, has_prev, has_next, "recv")
    px[...] = prior(xe[...], OWN, glob * OWN)
    load_basis().wait()
    pltpu.make_async_copy(obs_hbm, obs, ld_sem.at[0]).wait()

    def rs_core(k):
        return remote(rs_s.at[k], rs_r.at[k], rc_ss.at[k], rc_rs.at[k], sib)

    def rs_y(k):
        return remote(
            ry_s.at[k], ry_r.at[k], ry_ss.at[k], ry_rs.at[k], vdev((y + 4 - k) % 4, z, c)
        )

    @pl.loop(0, 4)
    def _(k):
        ag_c(0, k).wait_recv()
        yy = (y + 4 - k) % 4
        base = pl.multiple_of(yy * 256, 256)
        low = ag[0, yy].reshape(256, R)
        dacc[k] = jnp.zeros((256, R), F32)

        @pl.loop(0, 2)
        def _(jj):
            for u in range(2):
                cols = pl.ds(pl.multiple_of((jj * 2 + u) * 1024, 1024), 1024)
                b = basis[cols, :]
                prod = lax.dot_general(low, b, NT, preferred_element_type=F32)
                e = (prod - obs[pl.ds(base, 256), cols].astype(F32)).astype(BF) * mexp[
                    pl.ds(base, 256), cols
                ]
                dacc[k] += jnp.dot(e, b, preferred_element_type=F32)

        rs_s[k] = dacc[k, pl.ds(pl.multiple_of((1 - c) * 128, 128), 128), :].astype(BF)
        rs_core(k).start()

        @pl.when(k == 0)
        def _():
            for d in range(1, 4):
                ag_y_got(0, d).wait_recv()
                ag_c(0, d).start()
            expand(3)

        @pl.when(k >= 2)
        def _():
            rs_core(k - 1).wait_recv()
            ry_s[k - 1] = (
                dacc[k - 1, pl.ds(pl.multiple_of(c * 128, 128), 128), :]
                + rs_r[k - 1].astype(F32)
            ).astype(BF)
            rs_y(k - 1).start()

    rs_core(3).wait_recv()
    ry_s[3] = (
        dacc[3, pl.ds(pl.multiple_of(c * 128, 128), 128), :] + rs_r[3].astype(F32)
    ).astype(BF)
    rs_y(3).start()
    rs_core(0).wait_recv()
    part = dacc[0, pl.ds(pl.multiple_of(c * 128, 128), 128), :] + rs_r[0].astype(F32)
    for k in range(1, 4):
        rs_y(k).wait_recv()
        part = part + ry_r[k].astype(F32)
    zpart[...] = part * (2.0 ** -12)
    mine_rows = pl.ds(pl.multiple_of(z * 64, 64), 64)
    zpart[mine_rows, :] += px[...]
    rz_s[...] = zpart[...].astype(BF)
    rs_z = remote(rz_s, rz_r, rz_ss, rz_rs, zpeer)
    rs_z.start()
    rs_z.wait_recv()

    g128 = zpart[...] + rz_r[...].astype(F32)
    zpart[...] = g128
    ag[1, y, c] = g128.astype(BF).reshape(2, OWN, R)
    for d in range(1, 4):
        ag_y(1, d).start()
    ag_c(1, 0).start()
    for d in range(1, 4):
        ag_y_got(1, d).wait_recv()
        ag_c(1, d).start()
    for k in range(4):
        ag_c(1, k).wait_recv()
    ends(ghalo_copy, f > 0, f < 15, "start")
    def blocks(act):
        @pl.loop(0, 4)
        def _(yy):
            for cc in range(2):
                for zz in range(2):
                    frame = pl.multiple_of(yy * 256 + zz * 128 + cc * 64, 64)
                    place = pl.multiple_of(yy * 256 + cc * 128 + zz * 64, 64)
                    act(yy, cc, zz, frame, place)

    def widen(yy, cc, zz, frame, place):
        gfull[pl.ds(40 + frame, OWN), :] = ag[1, yy, cc, zz].astype(F32)

    blocks(widen)
    sub8 = lax.broadcasted_iota(jnp.int32, (1, 8, R), 1)

    def moved(turned, tiles):
        n = turned.shape[0] - 4
        a = jnp.where((tiles & 1) == 1, turned[1:], turned[:-1])
        a = jnp.where((tiles & 2) == 2, a[2:], a[:-2])
        return jnp.where(tiles == 4, turned[4:], a[:n]).reshape(n * 8, R)

    def earlier(window, lag):
        low = lag & 7
        turned = pltpu.roll(window, low, 1)
        near_rows = jnp.where(sub8 >= low, turned[1:], turned[:-1])
        return moved(near_rows, 4 - ((sub8 * 0 + lag) >> 3))

    def later(window, lag):
        low = lag & 7
        turned = pltpu.roll(window, (8 - low) & 7, 1)
        near_rows = jnp.where(sub8 < 8 - low, turned[:-1], turned[1:])
        return moved(near_rows, (sub8 * 0 + lag) >> 3)

    gfull[0:8] = jnp.zeros((8, R), F32)
    rbuf[1056:1064] = jnp.zeros((8, R), F32)

    @pl.loop(0, 11)
    def _(i):
        @pl.when(i == 9)
        def _():
            ends(ghalo_copy, f > 0, f < 15, "recv")
            gfull[8:40] = ghalo[0].astype(F32)
            gfull[1064:1096] = ghalo[1].astype(F32)

        at = pl.multiple_of((i + 1) % 11 * 96, 8)
        window = gfull[pl.ds(at, 136), :].reshape(17, 8, R)
        r = gfull[pl.ds(40 + at, 96), :]
        for l in range(NLAG):
            r = r - arw_ref[l : l + 1, :] * earlier(window, lag_ref[l])
        frame = f * ROWS + at + lax.broadcasted_iota(jnp.int32, (96, R), 0)
        rbuf[pl.ds(at, 96), :] = jnp.where((frame >= LAGMAX) & (frame < NF), r, 0.0)

    sums[...] = jnp.zeros_like(sums)

    @pl.loop(0, 8)
    def _(i):
        at = pl.multiple_of(i * 128, 128)
        window = rbuf[pl.ds(at, 168), :].reshape(21, 8, R)
        p = rbuf[pl.ds(at, 128), :]
        for l in range(NLAG):
            p = p - arw_ref[l : l + 1, :] * later(window, lag_ref[l])
        pgb[pl.ds(at, 128), :] = p
        g = gfull[pl.ds(40 + at, 128), :]
        for n, val in enumerate((g * g, g * p, p * p)):
            sums[n] += jnp.sum(val.reshape(16, 8, R), axis=0)

    lane = lax.broadcasted_iota(jnp.int32, (1, 128), 1)
    s1, s12, s2 = [
        jnp.sum(jnp.sum(sums[n], axis=0, keepdims=True), axis=1, keepdims=True) for n in range(3)
    ]
    row = jnp.where(
        lane == 0, s1, jnp.where(lane == 1, s12, jnp.where(lane == 2, s2, 0.0))
    )

    def exchange(val, slots, i, at, dev_of):
        mine[i] = val
        slots[at] = val
        for d in range(1, 4):
            remote(mine.at[i], slots.at[at], st_s.at[i], st_r.at[i], dev_of(d)).start()

        def whole():
            return remote(slots.at[pl.ds(0, 3)], slots.at[pl.ds(0, 3)], st_s.at[i], st_r.at[i], sib)

        whole().wait_recv()
        whole().wait_send()
        return jnp.sum(slots[...], axis=0)

    row = exchange(row, stat1, 0, x, lambda d: fdev(zl, (x + d) % 4))
    row = exchange(row, stat2, 1, zl, lambda d: fdev((zl + d) % 4, x))

    def pick(i):
        return jnp.sum(jnp.where(lane == i, row, 0.0), axis=1, keepdims=True)

    inv = 1.0 / (NF * R)
    ss1, s12, s22 = pick(0), pick(1), pick(2)
    b1 = 0.3 / jnp.sqrt(ss1 * inv + 1e-6)
    ss2 = jnp.maximum(ss1 - 2.0 * b1 * s12 + b1 * b1 * s22, 0.0)
    b2 = 0.3 / jnp.sqrt(ss2 * inv + 1e-6)
    by_g, by_p = b1 + b2, b1 * b2
    def step(yy, cc, zz, frame, place):
        low = ag[0, yy, cc, zz].astype(F32) - 0.0625 * (
            by_g * gfull[pl.ds(40 + frame, OWN), :] - by_p * pgb[pl.ds(frame, OWN), :]
        )
        cn[pl.ds(place, OWN), :] = low.astype(BF)

    blocks(step)

    @pl.loop(0, 4)
    def _(yy):
        at = pl.multiple_of(yy * 256, 256)
        ct[:, pl.ds(at, 256)] = cn[pl.ds(at, 256), :].T

    own_at = pl.multiple_of(v * OWN, OWN)
    newc_ref[...] = (
        coeff_ref[...] - by_g * zpart[mine_rows, :] + by_p * pgb[pl.ds(own_at, OWN), :]
    )

    def opp(w, s):
        half = pl.ds(s * 128, 128)
        return remote(
            s_opp.at[w, half], r_opp.at[w, half], opp_s.at[w, s], opp_rs.at[w, s],
            right if s == 0 else left,
        )

    def side(w, d, h):
        half = pl.ds(h * 128, 128)
        return remote(
            s_side.at[w, d, half], r_side.at[w, d, half],
            side_s.at[w, d, h], side_rs.at[w, d, h], right if d == 0 else left,
        )

    def two_blocks(w, xa, xb):
        def both(ref):
            return jnp.concatenate(
                [ref[:, pl.ds(pl.multiple_of(t * 1024 + w * WV, WV), WV)] for t in (xa, xb)], axis=1
            )

        b = jnp.concatenate(
            [basis[pl.ds(pl.multiple_of(t * 1024 + w * WV, WV), WV), :] for t in (xa, xb)], axis=0
        )
        prod = lax.dot_general(cn[...], b, NT, preferred_element_type=F32)
        e = (prod - both(obs).astype(F32)).astype(BF) * both(mexp)
        return jnp.dot(ct[...], e, preferred_element_type=F32)

    def compute(w):
        g = two_blocks(w, (x + 2) % 4, (x + 1) % 4)
        s_opp[w] = g[:, 0:WV].astype(BF)
        opp(w, 0).start()
        opp(w, 1).start()
        s_side[w, 0, 128:256] = g[128:256, WV:].astype(BF)
        side(w, 0, 1).start()
        gacc[w, 0] = g[0:128, WV:]
        g = two_blocks(w, (x + 3) % 4, x)
        s_side[w, 1, 0:128] = g[0:128, 0:WV].astype(BF)
        side(w, 1, 0).start()
        gacc[w, 1] = g[128:256, 0:WV]
        gown[w] = g[:, WV:]

    def join(w):
        opp(w, 0).wait_recv()
        s_side[w, 0, 0:128] = (gacc[w, 0] + r_opp[w, 0:128].astype(F32)).astype(BF)
        side(w, 0, 0).start()
        opp(w, 1).wait_recv()
        s_side[w, 1, 128:256] = (gacc[w, 1] + r_opp[w, 128:256].astype(F32)).astype(BF)
        side(w, 1, 1).start()

    def zsum(w, d):
        return remote(
            s_z.at[w, d], r_z.at[w, d], z_s.at[w, d], z_rs.at[w, d], fdev((zl + d) % 4, x)
        )

    def quarter(s):
        return (
            pl.ds(pl.multiple_of(s // 2 * SUB, SUB), SUB),
            pl.ds(pl.multiple_of(s % 2 * SUB, SUB), SUB),
        )

    def reduce_x(w):
        for d in range(2):
            for h in range(2):
                side(w, d, h).wait_recv()
        gown[w] = gown[w] + r_side[w, 0].astype(F32) + r_side[w, 1].astype(F32)
        for d in (2, 1, 3):
            ranks, verts = quarter((zl + d) % 4)
            s_z[w, d] = gown[w, ranks, verts].astype(BF)
            zsum(w, d).start()

    def quarter_of(w, s):
        return nb.at[s // 2, pl.ds(pl.multiple_of(x * 1024 + w * WV + s % 2 * SUB, SUB), SUB)]

    def block_of(w, xx):
        return nb.at[:, pl.ds(pl.multiple_of(xx * 1024 + w * WV, WV), WV)]

    def half_of(w, xx, t):
        return nb.at[t, pl.ds(pl.multiple_of(xx * 1024 + w * WV, WV), WV)]

    def gather_z(w, d):
        part = quarter_of(w, zl)
        return remote(part, part, az_s.at[w, d], az_r.at[w, d], fdev((zl + d) % 4, x))

    def gather_z_got(w, d):
        part = quarter_of(w, (zl + 4 - d) % 4)
        return remote(part, part, az_s.at[w, d], az_r.at[w, d], left)

    def gather_x(w, t):
        part = block_of(w, x)
        return remote(part, part, ax_s.at[w, t], ax_r.at[w, t], right if t == 0 else left)

    def gather_x_got(w, t):
        part = block_of(w, (x + (3 if t == 0 else 1)) % 4)
        return remote(part, part, ax_s.at[w, t], ax_r.at[w, t], left)

    def relay(w, t):
        part = half_of(w, (x + (3 if t == 0 else 1)) % 4, t)
        return remote(part, part, rel_s.at[w, t], rel_r.at[w, t], right if t == 0 else left)

    def relay_got(w, t):
        part = half_of(w, (x + 2) % 4, t)
        return remote(part, part, rel_s.at[w, t], rel_r.at[w, t], left)

    def store(w, xx, t):
        rows = pl.ds(xx * 1024 + w * WV, WV)
        return pltpu.make_async_copy(
            nb.at[t, rows], newb_hbm.at[rows, pl.ds(t * 128, 128)], out_sem.at[w, xx, t]
        )

    def update(w):
        ranks, verts = quarter(zl)
        acc = gown[w, ranks, verts]
        for d in range(1, 4):
            zsum(w, d).wait_recv()
            acc = acc + r_z[w, d].astype(F32)
        rows = pl.ds(pl.multiple_of(x * 1024 + w * WV + zl % 2 * SUB, SUB), SUB)
        nb[zl // 2, rows, :] = (
            basis[rows, ranks].astype(F32) - (2.0 ** -6) * acc.T
        ).astype(BF)
        for d in (2, 1, 3):
            gather_z(w, d).start()

    def spread(w):
        for d in range(1, 4):
            gather_z_got(w, d).wait_recv()
        gather_x(w, 0).start()
        gather_x(w, 1).start()

    def pass_on(w):
        for t in range(2):
            gather_x_got(w, t).wait_recv()
            relay(w, t).start()

    def finish(w):
        for t in range(2):
            relay_got(w, t).wait_recv()
        for xx in range(4):
            for t in range(2):
                store(w, xx, t).start()

    for act, w in (
        (compute, 0), (compute, 1), (join, 0), (compute, 2), (join, 1), (reduce_x, 0),
        (compute, 3), (join, 2), (update, 0), (reduce_x, 1), (join, 3), (spread, 0),
        (update, 1), (reduce_x, 2), (spread, 1), (reduce_x, 3), (update, 2), (pass_on, 0),
        (update, 3), (spread, 2), (pass_on, 1), (spread, 3), (finish, 0), (pass_on, 2),
        (finish, 1), (pass_on, 3), (finish, 2), (finish, 3),
    ):
        act(w)

    ag_z(0).wait_send()
    for i in range(2):
        for d in range(1, 4):
            ag_y(i, d).wait_send()
        for d in range(4):
            ag_c(i, d).wait_send()
    ends(halo, has_prev, has_next, "send")
    ends(ghalo_copy, f > 0, f < 15, "send")
    for k in range(4):
        rs_core(k).wait_send()
        if k:
            rs_y(k).wait_send()
    rs_z.wait_send()
    for w in range(WAVES):
        for t in range(2):
            opp(w, t).wait_send()
            for h in range(2):
                side(w, t, h).wait_send()
            gather_x(w, t).wait_send()
            relay(w, t).wait_send()
        for d in range(1, 4):
            zsum(w, d).wait_send()
            gather_z(w, d).wait_send()
    for w in range(WAVES):
        for xx in range(4):
            for t in range(2):
                store(w, xx, t).wait()


def shards(observed, mask, basis, coeffs, lag_set, ar_weight):
    vm = pltpu.VMEM
    dma = pltpu.SemaphoreType.DMA
    scratch = [
        vm((ROWS, COLS), BF),
        vm((32, ROWS), jnp.int32),
        vm((ROWS, COLS), BF),
        vm((COLS, R), BF),
        vm((2, 4, 2, 2, OWN, R), BF),
        vm((4, 256, R), F32),
        vm((4, 128, R), BF),
        vm((4, 128, R), BF),
        vm((4, 128, R), BF),
        vm((4, 128, R), BF),
        vm((128, R), BF),
        vm((128, R), BF),
        vm((128, R), F32),
        vm((128, R), F32),
        vm((OWN, R), F32),
        vm((ROWS + 72, R), F32),
        vm((2, 32, R), BF),
        vm((ROWS + 40, R), F32),
        vm((3, 8, R), F32),
        vm((ROWS, R), F32),
        vm((ROWS, R), BF),
        vm((4, 1, 128), F32),
        vm((4, 1, 128), F32),
        vm((2, 1, 128), F32),
        vm((R, ROWS), BF),
        vm((WAVES, 2, 128, WV), F32),
        vm((WAVES, R, WV), F32),
        vm((WAVES, R, WV), BF),
        vm((WAVES, R, WV), BF),
        vm((WAVES, 2, R, WV), BF),
        vm((WAVES, 2, R, WV), BF),
        vm((WAVES, 4, SUB, SUB), BF),
        vm((WAVES, 4, SUB, SUB), BF),
        vm((2, COLS, 128), BF),
        dma((3,)),
        dma((2,)), dma((2,)), dma((2, 4)), dma((2, 4)), dma((2, 4)), dma((2, 4)),
        dma((2,)), dma((2,)), dma((2,)), dma((2,)),
        dma((4,)), dma((4,)), dma((4,)), dma((4,)), dma, dma,
        dma((2,)), dma((2,)),
        dma((WAVES, 2)), dma((WAVES, 2)), dma((WAVES, 2, 2)), dma((WAVES, 2, 2)),
        dma((WAVES, 4)), dma((WAVES, 4)), dma((WAVES, 4)), dma((WAVES, 4)),
        dma((WAVES, 2)), dma((WAVES, 2)), dma((WAVES, 2)), dma((WAVES, 2)),
        dma((WAVES, 4, 2)),
    ]
    anyspace = pl.BlockSpec(memory_space=pl.ANY)
    vmem = pl.BlockSpec(memory_space=pltpu.VMEM)
    return pl.pallas_call(
        kernel,
        out_shape=(
            jax.ShapeDtypeStruct((OWN, R), F32),
            jax.ShapeDtypeStruct((COLS, R), BF),
        ),
        in_specs=[anyspace, anyspace, anyspace, vmem, pl.BlockSpec(memory_space=pltpu.SMEM), vmem],
        out_specs=(vmem, anyspace),
        scratch_shapes=scratch,
        compiler_params=pltpu.CompilerParams(
            collective_id=0, has_side_effects=True, vmem_limit_bytes=60 * 2**20
        ),
        name="alternation",
    )(observed, mask.T, basis, coeffs, lag_set, ar_weight)


def solution(mesh):
    placed = (
        P("frames", "verts"),
        P("frames", "verts"),
        P("verts", None),
        P(("frames", "verts"), None),
        P(),
        P(),
    )
    return jax.shard_map(
        shards,
        mesh=mesh,
        in_specs=placed,
        out_specs=(P(("frames", "verts"), None), P("verts", None)),
        check_vma=False,
    )
```
